32 devices in a mesh: grp: 8 (over z, x), blk: 4 (over y, core).
Axes of the slice: x: 2, y: 2, z: 4, core: 2. Of those that a mesh axis runs over, the one named last changes fastest.
Arguments:
- embeddings: bfloat16 [49152, 768], P(('grp', 'blk')), may hold values from -6 to 6
- route: int32 [49152], P(('grp', 'blk')), may hold values from 0 to 49151, as said below
- cluster: int32 [8, 6144], P('grp', 'blk'), may hold values from 0 to 3, never falling along the last dimension, each value on 1 to 3072 neighbouring positions
Outputs:
- best_cosine: float32 [49152], P(('grp', 'blk'))
The draws below stay inside these ranges and needn't reach their ends.
Inputs may be any that keep to these rules, and one draw needn't show every extreme that they name: route is a permutation of all slots; the 1536 rows of each device are sent to every device's 1536 slots in exactly 48 cases, and which rows and which slots is drawn from the seed. Within each family the cluster numbers never fall along the slots, every cluster number occurs, and one cluster has exactly 3072 slots.
All inputs are finite; a program needn't handle non-finite values.
Results may differ from the reference program's by a relative error of at most 0.0014.
Values may be sent and summed in bfloat16 or wider, within the bound.
No kernel may reach another device: no remote copies, remote signals or barrier semaphores. Data moves between devices by JAX's collectives and lax.ppermute only.
A program may use at most 64 MiB of HBM per device.

```python
import math
import jax
import jax.numpy as jnp
import numpy as np
from jax import lax

D = 768
ROW_DEV = 1536
CLUSTERS_GRP = 4
GROUP_ROWS = 6144
MOST = 3072
ROWS = 49152
N_GRP = 8


def draw_route(key, part):
    device_count = ROWS // ROW_DEV
    pair_rows = ROW_DEV // device_count
    source_keys = jax.random.split(jax.random.fold_in(key, 11), device_count)
    target_keys = jax.random.split(jax.random.fold_in(key, 12), device_count)
    source_perm = jax.vmap(lambda piece: jax.random.permutation(piece, ROW_DEV))(source_keys).astype(jnp.int32)
    target_perm = jax.vmap(lambda piece: jax.random.permutation(piece, ROW_DEV))(target_keys).astype(jnp.int32)
    destination = source_perm // pair_rows
    within_pair = source_perm % pair_rows
    sources = jnp.arange(device_count, dtype=jnp.int32)[:, None]
    slot_pos = target_perm[destination, sources * pair_rows + within_pair]
    return (destination * ROW_DEV + slot_pos).reshape(-1).astype(jnp.int32)


def block_scale(rng, extent, cuts, low, largest):
    loudness, own = 1.0, jax.random.fold_in(rng, 6)
    for dim, blocks in cuts:
        draws = jnp.exp(jax.random.uniform(jax.random.fold_in(own, dim), (blocks,), jnp.float32, low / len(cuts), largest / len(cuts)))
        loudness = loudness * jnp.repeat(draws, extent[dim] // blocks).reshape([-1 if axis == dim else 1 for axis in range(len(extent))])
    return loudness


def profile(number_of, total, limit, slope):
    weights = [(1 << 20) // math.isqrt(standing ** slope) + 1 for standing in range(2, number_of + 1)]
    surplus, given = total - limit - (number_of - 1), [1] * (number_of - 1)
    while surplus > 0:
        candidates = [i for i in range(number_of - 1) if given[i] < limit]
        pool, left = sum([weights[i] for i in candidates]), surplus
        for i in candidates:
            addition = min(limit - given[i], max(1, left * weights[i] // pool), surplus)
            given[i] = given[i] + addition
            surplus = surplus - addition
    return np.array([limit] + given)


def uneven_parts(key, count, total, reach, skew):
    if count == 2:
        one = jax.random.randint(key, (), max(1, total - reach), min(reach, total - 1) + 1)
        return jnp.stack([one, total - one])
    lengths = jnp.asarray(profile(count, total, reach, skew), jnp.int32)
    twos = (count - 1) // 2
    donor, receiver = lengths[1:1 + 2 * twos:2], lengths[2:2 + 2 * twos:2]
    margin = jnp.minimum(donor - 1, reach - receiver)
    moved = jax.random.randint(jax.random.fold_in(key, 1), (twos,), 0, 1 << 20) % (margin + 1)
    lengths = lengths.at[1:1 + 2 * twos:2].set(donor - moved).at[2:2 + 2 * twos:2].set(receiver + moved)
    return lengths[jax.random.permutation(jax.random.fold_in(key, 2), count)]


def bell_draw(own_key, shape, width, most, cuts=(), kind=jnp.bfloat16):
    array = width * jax.random.normal(own_key, shape, jnp.float32)
    if cuts:
        array = array * block_scale(own_key, shape, cuts, -0.22, 0.18)
    return jnp.clip(array, -most, most).astype(kind)


def setup_inputs(seed: int = 0) -> dict:
    arg_keys = jax.random.split(jax.random.key(seed), 4)
    return {
        "embeddings": bell_draw(arg_keys[0], (ROWS, D), 1.0, 6.0, ((0, 32),)),
        "route": draw_route(jax.random.fold_in(arg_keys[3], 71), 0),
        "cluster": jax.vmap(lambda own: jnp.searchsorted(jnp.cumsum(uneven_parts(own, CLUSTERS_GRP, GROUP_ROWS, MOST, 2)), jnp.arange(GROUP_ROWS), side="right"))(jax.random.split(arg_keys[2], N_GRP)).reshape((N_GRP, GROUP_ROWS)).astype(jnp.int32),
    }


def family_scores(group_unit, group_index, group_cluster):
    total_rows = group_unit.shape[0]
    block_rows = 512 if total_rows % 512 == 0 else total_rows

    def one_block(start):
        unit_part = lax.dynamic_slice_in_dim(group_unit, start, block_rows, 0)
        index_part = lax.dynamic_slice_in_dim(group_index, start, block_rows, 0)
        cluster_part = lax.dynamic_slice_in_dim(group_cluster, start, block_rows, 0)
        scores = jnp.dot(unit_part, group_unit.T, preferred_element_type=jnp.float32)
        matches = (cluster_part[:, None] == group_cluster[None, :]) & (group_index[None, :] < index_part[:, None])
        floor_value = jnp.full(scores.shape, -1.0, scores.dtype)
        return lax.optimization_barrier(jnp.max(jnp.where(matches, scores, floor_value), axis=1))
    starts = jnp.arange(total_rows // block_rows, dtype=jnp.int32) * block_rows
    return lax.map(one_block, starts).reshape(total_rows)

def reference(embeddings, route, cluster):
    values = embeddings.astype(jnp.float32)
    unit_rows = (values * lax.rsqrt(lax.optimization_barrier(jnp.sum(values * values, axis=1, keepdims=True)) + 1e-06)).astype(jnp.bfloat16)
    positions = jnp.arange(ROWS, dtype=jnp.int32)
    slot_unit = jnp.zeros_like(unit_rows).at[route].set(unit_rows)
    slot_index = jnp.zeros((ROWS,), jnp.int32).at[route].set(positions)
    slot_best = lax.map(lambda packed: family_scores(packed[0], packed[1], packed[2]), (slot_unit.reshape(N_GRP, GROUP_ROWS, D), slot_index.reshape(N_GRP, GROUP_ROWS), cluster))
    return slot_best.reshape(ROWS)[route]
```

```python
import functools

import jax
import jax.numpy as jnp
from jax import lax
from jax.experimental import pallas as pl
from jax.experimental.pallas import tpu as pltpu
from jax.sharding import PartitionSpec as P

BF16, F32, I32 = jnp.bfloat16, jnp.float32, jnp.int32
LANES = 128
CLUSTERS = 4
VMEM = pl.BlockSpec(memory_space=pltpu.VMEM)
SMEM = pl.BlockSpec(memory_space=pltpu.SMEM)
ANY = pl.BlockSpec(memory_space=pl.ANY)
MIB = 1 << 20


def dot_nt(a, b):
    return lax.dot_general(a, b, (((1,), (1,)), ((), ())), preferred_element_type=F32)


def iota(shape, dim):
    return lax.broadcasted_iota(I32, shape, dim)


def one_hot(match):
    return jnp.where(match, 1.0, 0.0).astype(BF16)


def place_kernel(n, piece, family_rows, route_ref, cluster_ref, fam_ref, rank_ref, meta_ref):
    blocks = route_ref.shape[0]
    route = route_ref[...]
    fam = jnp.zeros_like(route)
    for f in range(1, n):
        fam = fam + jnp.where(route >= f * family_rows, 1, 0)
    rel = route - fam * family_rows
    pad = 16 - blocks % 16 if blocks % 16 else 0
    tall = blocks + pad
    fam_pad = jnp.concatenate([fam, jnp.full((pad, LANES), -1, I32)], axis=0) if pad else fam
    member = jnp.concatenate(
        [jnp.where(fam_pad == f, 1.0, 0.0) for f in range(n)], axis=0
    )
    member_low = member.astype(BF16)
    before = one_hot(iota((LANES, LANES), 0) < iota((LANES, LANES), 1))
    within = jnp.dot(member_low, before, preferred_element_type=F32)
    totals = jnp.dot(member_low, jnp.ones((LANES, LANES), BF16), preferred_element_type=F32)
    size = n * tall
    shift = tall.bit_length() - 1
    row, col = iota((size, size), 0), iota((size, size), 1)
    above = one_hot(((row >> shift) == (col >> shift)) & (col < row))
    ranks = within + jnp.dot(above, totals.astype(BF16), preferred_element_type=F32)
    ranks = ranks * member
    rank = jnp.zeros((tall, LANES), F32)
    for f in range(n):
        rank = rank + ranks[f * tall:(f + 1) * tall]
    rank = rank.astype(I32)

    def as_row(x):
        return jnp.concatenate([x[i:i + 1] for i in range(blocks)], axis=1)

    fam_row, rank_row, rel_row = as_row(fam), as_row(rank), as_row(rel)
    fam_ref[...] = fam_row
    rank_ref[...] = rank_row
    rows = fam_row.shape[1]
    mine = iota((n, rows), 0) == fam_row
    high = jnp.where(mine, (rel_row >> 6).astype(F32), 0.0)
    low = jnp.where(mine, (rel_row & 63).astype(F32), 0.0)
    at_rank = one_hot(iota((piece, rows), 0) == rank_row)
    packed = dot_nt(jnp.concatenate([high, low], axis=0).astype(BF16), at_rank)
    slots = packed[:n] * 64.0 + packed[n:]
    meta_ref[:n] = slots.astype(I32)
    cluster = cluster_ref[...]
    lane = iota((8, piece), 1)
    counts = jnp.zeros((8, piece), F32)
    for c in range(CLUSTERS - 1):
        counts = jnp.where(lane == c, jnp.sum(jnp.where(cluster <= c, 1.0, 0.0)), counts)
    meta_ref[n:] = counts.astype(I32)


def pack_kernel(n, piece, here_ref, emb_ref, fam_ref, rank_ref, *rest):
    outs, unit_ref = rest[:n], rest[n]
    rows, _ = emb_ref.shape
    grp = here_ref[0]

    @pl.loop(0, rows // 128)
    def _(i):
        at = pl.ds(pl.multiple_of(i * 128, 128), 128)
        x = emb_ref[at, :].astype(F32)
        total = jnp.sum(x * x, axis=1, keepdims=True)
        unit_ref[at, :] = (x * lax.rsqrt(total + 1e-06)).astype(BF16)

    pos = (fam_ref[...] ^ grp) * piece + rank_ref[...]
    group = max(1, min(n, 384 // piece))
    for start in range(0, n, group):
        select = one_hot(iota((group * piece, rows), 0) + start * piece == pos)
        got = jnp.dot(select, unit_ref[...], preferred_element_type=F32).astype(BF16)
        for i in range(group):
            outs[start + i][...] = got[i * piece:(i + 1) * piece]


def score_kernel(n, nb, piece, here_ref, left_ref, right_ref, kcl_ref, qcl_ref, *rest):
    pieces = [rest[d * nb:(d + 1) * nb] for d in range(n)]
    out_ref, keys, best, sems = rest[n * nb:]
    grp, blk = here_ref[0], here_ref[1]
    width = keys.shape[-1]
    copies = []
    for d in range(n):
        for e in range(nb):
            copy = pltpu.make_async_copy(
                pieces[d][e], keys.at[grp ^ d, blk ^ e], sems.at[d, e]
            )
            copy.start()
            copies.append(copy)
    best[...] = jnp.full(best.shape, -1.0, F32)
    for copy in copies:
        copy.wait()
    span = nb * piece

    def fold(query, key, causal):
        q = keys[query, blk]
        k = keys[key].reshape(span, width)
        scores = dot_nt(k, q)
        match = kcl_ref[key] == qcl_ref[query]
        if causal:
            match = match & (iota((span, piece), 0) < blk * piece + iota((span, piece), 1))
        scores = jnp.where(match, scores, -1.0)
        best[query] = jnp.maximum(best[query], jnp.max(scores.reshape(span // 8, 8, piece), axis=0))

    @pl.loop(0, n)
    def _(i):
        fold(i, i, True)

    @pl.loop(0, left_ref.shape[0])
    def _(i):
        one, two = grp ^ left_ref[i], grp ^ right_ref[i]
        fold(jnp.maximum(one, two), jnp.minimum(one, two), False)

    for i in range(n):
        out_ref[i:i + 1] = jnp.max(best[i], axis=0, keepdims=True)


def unpack_kernel(n, piece, score_ref, fam_ref, rank_ref, out_ref):
    x = score_ref[...]
    high = x.astype(BF16)
    rest = x - high.astype(F32)
    mid = rest.astype(BF16)
    low = (rest - mid.astype(F32)).astype(BF16)
    rows = fam_ref.shape[1]
    at_rank = one_hot(iota((piece, rows), 0) == rank_ref[...])
    got = jnp.dot(jnp.concatenate([high, mid, low], axis=0), at_rank, preferred_element_type=F32)
    value = got[:n] + got[n:2 * n] + got[2 * n:]
    value = jnp.where(iota((n, rows), 0) == fam_ref[...], value, 0.0)
    out_ref[...] = jnp.sum(value, axis=0, keepdims=True)


def shape(*dims, kind=F32):
    return jax.ShapeDtypeStruct(dims, kind)


def send(x, axis, by):
    return lax.ppermute(x, axis, [(i, i ^ by) for i in range(lax.axis_size(axis))])


def on_device(embeddings, route, cluster):
    rows, width = embeddings.shape
    n, nb = lax.axis_size("grp"), lax.axis_size("blk")
    piece = rows // n
    family_rows = rows * nb
    grp, blk = lax.axis_index("grp"), lax.axis_index("blk")
    here = jnp.stack([grp, blk]).astype(I32)
    blocks = rows // LANES

    fam, rank, meta = pl.pallas_call(
        functools.partial(place_kernel, n, piece, family_rows),
        out_shape=[shape(1, rows, kind=I32), shape(1, rows, kind=I32), shape(n + 8, piece, kind=I32)],
        in_specs=[VMEM] * 2,
        out_specs=[VMEM] * 3,
        compiler_params=pltpu.CompilerParams(vmem_limit_bytes=32 * MIB),
        name="place",
    )(route.reshape(blocks, LANES), cluster.reshape(blocks, LANES))

    sent = pl.pallas_call(
        functools.partial(pack_kernel, n, piece),
        out_shape=[shape(piece, width, kind=BF16)] * n,
        in_specs=[SMEM, VMEM, VMEM, VMEM],
        out_specs=[VMEM] * n,
        scratch_shapes=[pltpu.VMEM((rows, width), BF16)],
        compiler_params=pltpu.CompilerParams(vmem_limit_bytes=48 * MIB),
        name="pack",
    )(here, embeddings, fam, rank)

    everyone = lax.all_gather(meta, ("grp", "blk"))
    slots = lax.dynamic_index_in_dim(everyone[:, :n], grp, 1, keepdims=False)
    counts = lax.dynamic_slice_in_dim(everyone[:, n, :CLUSTERS - 1], grp * nb, nb, 0)
    bounds = jnp.sum(counts, axis=0)
    kinds = jnp.zeros_like(slots)
    for c in range(CLUSTERS - 1):
        kinds = kinds + (slots >= bounds[c]).astype(I32)
    kinds = kinds.reshape(n, nb, piece)
    query_kinds = lax.dynamic_index_in_dim(kinds, blk, 1, keepdims=True)
    key_kinds = kinds.reshape(n, nb * piece, 1)

    order = sorted(range(n), key=lambda d: -d)
    held = [None] * n
    for d in order:
        own = sent[d] if d == 0 else send(sent[d], "grp", d)
        held[d] = [own]
    for d in reversed(order):
        across = send(held[d][0], "blk", 2)
        held[d] += [send(held[d][0], "blk", 1), across, send(across, "blk", 1)]

    pairs = [(a, b) for a in range(n) for b in range(a)]
    left = jnp.array([a for a, _ in pairs], I32)
    right = jnp.array([b for _, b in pairs], I32)
    best = pl.pallas_call(
        functools.partial(score_kernel, n, nb, piece),
        out_shape=shape(n, piece),
        in_specs=[SMEM] * 3 + [VMEM] * 2 + [ANY] * (n * nb),
        out_specs=VMEM,
        scratch_shapes=[
            pltpu.VMEM((n, nb, piece, width), BF16),
            pltpu.VMEM((n, 8, piece), F32),
            pltpu.SemaphoreType.DMA((n, nb)),
        ],
        compiler_params=pltpu.CompilerParams(vmem_limit_bytes=48 * MIB),
        name="score",
    )(here, left, right, key_kinds, query_kinds, *[p for group in held for p in group])

    home = lax.all_to_all(best, "grp", split_axis=0, concat_axis=0, tiled=True)
    out = pl.pallas_call(
        functools.partial(unpack_kernel, n, piece),
        out_shape=shape(1, rows),
        in_specs=[VMEM] * 3,
        out_specs=VMEM,
        compiler_params=pltpu.CompilerParams(vmem_limit_bytes=32 * MIB),
        name="unpack",
    )(home, fam, rank)
    return out.reshape(rows)


def solution(mesh):
    in_specs = (P(("grp", "blk"), None), P(("grp", "blk")), P("grp", "blk"))
    return jax.shard_map(
        on_device, mesh=mesh, in_specs=in_specs, out_specs=P(("grp", "blk")), check_vma=False
    )
```

```python
import functools

import jax
import jax.numpy as jnp
from jax import lax
from jax.experimental import pallas as pl
from jax.experimental.pallas import tpu as pltpu
from jax.sharding import PartitionSpec as P

BF16, F32, I32 = jnp.bfloat16, jnp.float32, jnp.int32
LANES = 128
CLUSTERS = 4
VMEM = pl.BlockSpec(memory_space=pltpu.VMEM)
SMEM = pl.BlockSpec(memory_space=pltpu.SMEM)
ANY = pl.BlockSpec(memory_space=pl.ANY)
MIB = 1 << 20


def dot_nt(a, b):
    return lax.dot_general(a, b, (((1,), (1,)), ((), ())), preferred_element_type=F32)


def iota(shape, dim):
    return lax.broadcasted_iota(I32, shape, dim)


def one_hot(match):
    return jnp.where(match, 1.0, 0.0).astype(BF16)


def place_kernel(n, nb, piece, family_rows, route_ref, cluster_ref, fam_ref, rank_ref, meta_ref):
    blocks = route_ref.shape[0]
    route = route_ref[...]
    fam = jnp.zeros_like(route)
    for f in range(1, n):
        fam = fam + jnp.where(route >= f * family_rows, 1, 0)
    rel = route - fam * family_rows
    pad = 16 - blocks % 16 if blocks % 16 else 0
    tall = blocks + pad
    fam_pad = jnp.concatenate([fam, jnp.full((pad, LANES), -1, I32)], axis=0) if pad else fam
    member = jnp.concatenate(
        [jnp.where(fam_pad == f, 1.0, 0.0) for f in range(n)], axis=0
    )
    member_low = member.astype(BF16)
    before = one_hot(iota((LANES, LANES), 0) < iota((LANES, LANES), 1))
    within = jnp.dot(member_low, before, preferred_element_type=F32)
    totals = jnp.dot(member_low, jnp.ones((LANES, LANES), BF16), preferred_element_type=F32)
    size = n * tall
    shift = tall.bit_length() - 1
    row, col = iota((size, size), 0), iota((size, size), 1)
    above = one_hot(((row >> shift) == (col >> shift)) & (col < row))
    ranks = within + jnp.dot(above, totals.astype(BF16), preferred_element_type=F32)
    ranks = ranks * member
    rank = jnp.zeros((tall, LANES), F32)
    for f in range(n):
        rank = rank + ranks[f * tall:(f + 1) * tall]
    rank = rank.astype(I32)

    def as_row(x):
        return jnp.concatenate([x[i:i + 1] for i in range(blocks)], axis=1)

    fam_row, rank_row, rel_row = as_row(fam), as_row(rank), as_row(rel)
    fam_ref[...] = fam_row
    rank_ref[...] = rank_row
    rows = fam_row.shape[1]
    mine = iota((n, rows), 0) == fam_row
    high = jnp.where(mine, (rel_row >> 6).astype(F32), 0.0)
    low = jnp.where(mine, (rel_row & 63).astype(F32), 0.0)
    at_rank = one_hot(iota((piece, rows), 0) == rank_row)
    packed = dot_nt(jnp.concatenate([high, low], axis=0).astype(BF16), at_rank)
    slots = packed[:n] * 64.0 + packed[n:]
    cluster = cluster_ref[...]
    wide = meta_ref.shape[-1]
    lane = iota((n, wide - piece), 1)
    counts = jnp.zeros((n, wide - piece), F32)
    for c in range(CLUSTERS - 1):
        counts = jnp.where(lane == c, jnp.sum(jnp.where(cluster <= c, 1.0, 0.0)), counts)
    meta = jnp.concatenate([slots, counts], axis=1).astype(I32)
    for f in range(n):
        for e in range(nb):
            meta_ref[f * nb + e] = meta[f:f + 1]


def pack_kernel(n, piece, here_ref, emb_ref, fam_ref, rank_ref, *rest):
    outs, unit_ref = rest[:n], rest[n]
    rows, _ = emb_ref.shape
    grp = here_ref[0]

    @pl.loop(0, rows // 128)
    def _(i):
        at = pl.ds(pl.multiple_of(i * 128, 128), 128)
        x = emb_ref[at, :].astype(F32)
        total = jnp.sum(x * x, axis=1, keepdims=True)
        unit_ref[at, :] = (x * lax.rsqrt(total + 1e-06)).astype(BF16)

    pos = (fam_ref[...] ^ grp) * piece + rank_ref[...]
    group = max(1, min(n, 384 // piece))
    for start in range(0, n, group):
        select = one_hot(iota((group * piece, rows), 0) + start * piece == pos)
        got = jnp.dot(select, unit_ref[...], preferred_element_type=F32).astype(BF16)
        for i in range(group):
            outs[start + i][...] = got[i * piece:(i + 1) * piece]


def kinds_kernel(n, nb, piece, here_ref, meta_ref, key_ref, query_ref):
    grp, blk = here_ref[0], here_ref[1]
    wide = meta_ref.shape[-1]
    counts = meta_ref[grp * nb]
    for e in range(1, nb):
        counts = counts + meta_ref[grp * nb + e]
    lane = iota((1, wide), 1)
    bounds = [
        jnp.sum(jnp.where(lane == piece + c, counts, 0).astype(F32)) for c in range(CLUSTERS - 1)
    ]
    first = iota((8, piece), 0) == 0
    ones = jnp.where(iota((8, LANES), 0) == 0, 1.0, 0.0).astype(BF16)

    def kinds(source):
        slots = meta_ref[source].astype(F32)[:, :piece]
        total = jnp.zeros_like(slots)
        for bound in bounds:
            total = total + jnp.where(slots >= bound, 1.0, 0.0)
        return total

    @pl.loop(0, n * nb)
    def _(source):
        tall = jnp.where(first, kinds(source), 0.0).astype(BF16)
        key_ref[source] = lax.dot_general(
            tall, ones, (((0,), (0,)), ((), ())), preferred_element_type=F32
        )

    @pl.loop(0, n)
    def _(i):
        query_ref[i] = kinds(i * nb + blk)


def stage_kernel(n, nb, piece, lo, hi, here_ref, kcl_ref, qcl_ref, *rest):
    count = hi - lo
    pieces = [rest[i * nb:(i + 1) * nb] for i in range(count)]
    rest = rest[count * nb + (2 if lo else 0):]
    if hi < n:
        keys, best = rest
    else:
        outs, (keys, best) = rest[:n], rest[n:]
    grp, blk = here_ref[0], here_ref[1]
    width = keys.shape[-1]
    span = nb * piece
    if not lo:
        best[...] = jnp.full(best.shape, -1.0, F32)
    for i in range(count):
        for e in range(nb):
            keys[grp ^ (lo + i), blk ^ e] = pieces[i][e][...]

    def fold(query, key, causal):
        q = keys[query, blk]
        k = keys[key].reshape(span, width)
        scores = dot_nt(k, q)
        kinds = kcl_ref[pl.ds(key * nb, nb)].reshape(span, LANES)
        parts = []
        for at in range(0, piece, LANES):
            w = min(LANES, piece - at)
            match = kinds[:, :w] == qcl_ref[query][:, at:at + w]
            if causal:
                early = iota((span, w), 0) - iota((span, w), 1) < blk * piece + at
                match = match & early
            part = jnp.where(match, scores[:, at:at + w], -1.0)
            parts.append(jnp.max(part.reshape(span // 8, 8, w), axis=0))
        folded = jnp.concatenate(parts, axis=1) if len(parts) > 1 else parts[0]
        best[query] = jnp.maximum(best[query], folded)

    @pl.loop(lo, hi)
    def _(a):
        one = grp ^ a
        fold(one, one, True)

        @pl.loop(0, a)
        def _(b):
            two = grp ^ b
            fold(jnp.maximum(one, two), jnp.minimum(one, two), False)

    if hi == n:
        for d in range(n):
            outs[d][...] = jnp.max(best[grp ^ d], axis=0, keepdims=True)


def unpack_kernel(n, piece, here_ref, fam_ref, rank_ref, *rest):
    scores, out_ref = rest[:n], rest[n]
    x = jnp.concatenate([r[...] for r in scores], axis=0)
    high = x.astype(BF16)
    rest = x - high.astype(F32)
    mid = rest.astype(BF16)
    low = (rest - mid.astype(F32)).astype(BF16)
    rows = fam_ref.shape[1]
    at_rank = one_hot(iota((piece, rows), 0) == rank_ref[...])
    got = jnp.dot(jnp.concatenate([high, mid, low], axis=0), at_rank, preferred_element_type=F32)
    value = got[:n] + got[n:2 * n] + got[2 * n:]
    value = jnp.where(iota((n, rows), 0) == (fam_ref[...] ^ here_ref[0]), value, 0.0)
    out_ref[...] = jnp.sum(value, axis=0, keepdims=True)


def shape(*dims, kind=F32):
    return jax.ShapeDtypeStruct(dims, kind)


def send(x, axis, by):
    return lax.ppermute(x, axis, [(i, i ^ by) for i in range(lax.axis_size(axis))])


def after(x, *deps):
    return lax.optimization_barrier((x,) + deps)[0]


def limit(mib):
    return pltpu.CompilerParams(vmem_limit_bytes=mib * MIB)


def on_device(embeddings, route, cluster):
    rows, width = embeddings.shape
    n, nb = lax.axis_size("grp"), lax.axis_size("blk")
    piece = rows // n
    grp, blk = lax.axis_index("grp"), lax.axis_index("blk")
    here = jnp.stack([grp, blk]).astype(I32)
    blocks = rows // LANES
    wide = -(-(piece + CLUSTERS - 1) // LANES) * LANES

    fam, rank, meta = pl.pallas_call(
        functools.partial(place_kernel, n, nb, piece, rows * nb),
        out_shape=[shape(1, rows, kind=I32)] * 2 + [shape(n * nb, 1, wide, kind=I32)],
        in_specs=[VMEM] * 2,
        out_specs=[VMEM] * 3,
        compiler_params=limit(16),
        name="place",
    )(route.reshape(blocks, LANES), cluster.reshape(blocks, LANES))

    sent = pl.pallas_call(
        functools.partial(pack_kernel, n, piece),
        out_shape=[shape(piece, width, kind=BF16)] * n,
        in_specs=[SMEM, VMEM, VMEM, VMEM],
        out_specs=[VMEM] * n,
        scratch_shapes=[pltpu.VMEM((rows, width), BF16)],
        compiler_params=limit(16),
        name="pack",
    )(here, embeddings, fam, rank)

    held = [None] * n
    def spread(own, across):
        return [own, send(own, "blk", 1), across, send(across, "blk", 1)]

    half = n // 2
    across = [None] * n
    own = [sent[0]] + [None] * (n - 1)
    own[half] = send(sent[half], "grp", half)
    own[half + 1] = send(sent[half + 1], "grp", half + 1)
    across[0] = send(own[0], "blk", 2)
    for d in range(1, half):
        own[d] = send(sent[d] if d < 3 else after(sent[d], own[d - 2]), "grp", d)
    for d in range(half + 2, n):
        own[d] = send(after(sent[d], own[d - 1 if d > half + 2 else half]), "grp", d)
    for d in range(1, n):
        across[d] = send(own[d] if d < 2 else after(own[d], across[d - 2]), "blk", 2)
    held = [spread(own[d], across[d]) for d in range(n)]

    heard = lax.all_to_all(
        after(meta, own[1]), ("grp", "blk"), split_axis=0, concat_axis=0, tiled=True
    )
    key_kinds, query_kinds = pl.pallas_call(
        functools.partial(kinds_kernel, n, nb, piece),
        out_shape=[shape(n * nb, piece, LANES), shape(n, 1, piece)],
        in_specs=[SMEM, VMEM],
        out_specs=[VMEM] * 2,
        compiler_params=limit(16),
        name="kinds",
    )(here, heard)

    cuts = [0, half, half + 2, half + 3, n] if n == 8 else list(range(0, n + 1, 8))
    state = []
    for lo, hi in zip(cuts, cuts[1:]):
        last = hi == n
        kept = [shape(n, nb, piece, width, kind=BF16), shape(n, 8, piece)]
        folds = sum(d + 1 for d in range(lo, hi))
        args = [here, key_kinds, query_kinds] + [p for d in range(lo, hi) for p in held[d]] + list(state)
        state = pl.pallas_call(
            functools.partial(stage_kernel, n, nb, piece, lo, hi),
            out_shape=([shape(1, piece)] * n if last else []) + kept,
            in_specs=[SMEM] + [VMEM] * (len(args) - 1),
            out_specs=[VMEM] * ((n if last else 0) + 2),
            input_output_aliases={
                len(args) - 2 + i: (n if last else 0) + i for i in range(2)
            } if lo else {},
            compiler_params=limit(12),
            cost_estimate=pl.CostEstimate(
                flops=folds * 2 * piece * piece * nb * width, bytes_accessed=0, transcendentals=0
            ),
            name="stage",
        )(*args)
    best = state[:n]

    home = [best[0]] + [send(best[d], "grp", d) for d in range(1, n)]
    out = pl.pallas_call(
        functools.partial(unpack_kernel, n, piece),
        out_shape=shape(1, rows),
        in_specs=[SMEM] + [VMEM] * (2 + n),
        out_specs=VMEM,
        compiler_params=limit(16),
        name="unpack",
    )(here, fam, rank, *home)
    return out.reshape(rows)


def solution(mesh):
    in_specs = (P(("grp", "blk"), None), P(("grp", "blk")), P("grp", "blk"))
    return jax.shard_map(
        on_device, mesh=mesh, in_specs=in_specs, out_specs=P(("grp", "blk")), check_vma=False
    )
```

```python
import functools

import jax
import jax.numpy as jnp
from jax import lax
from jax.experimental import pallas as pl
from jax.experimental.pallas import tpu as pltpu
from jax.sharding import PartitionSpec as P

BF16, F32, I32 = jnp.bfloat16, jnp.float32, jnp.int32
LANES = 128
CLUSTERS = 4
NOTE = 8
VMEM = pl.BlockSpec(memory_space=pltpu.VMEM)
SMEM = pl.BlockSpec(memory_space=pltpu.SMEM)
ANY = pl.BlockSpec(memory_space=pl.ANY)
MIB = 1 << 20


def dot_nt(a, b):
    return lax.dot_general(a, b, (((1,), (1,)), ((), ())), preferred_element_type=F32)


def iota(shape, dim):
    return lax.broadcasted_iota(I32, shape, dim)


def one_hot(match):
    return jnp.where(match, 1.0, 0.0).astype(BF16)


def digits(x):
    return [(x >> 6).astype(F32), (x & 63).astype(F32)]


def places(n, family_rows, route):
    blocks = route.shape[0]
    fam = jnp.zeros_like(route)
    for f in range(1, n):
        fam = fam + jnp.where(route >= f * family_rows, 1, 0)
    rel = route - fam * family_rows
    pad = -blocks % 16
    tall = blocks + pad
    fam_pad = jnp.concatenate([fam, jnp.full((pad, LANES), -1, I32)], axis=0) if pad else fam
    member = jnp.concatenate([jnp.where(fam_pad == f, 1.0, 0.0) for f in range(n)], axis=0)
    member_low = member.astype(BF16)
    before = one_hot(iota((LANES, LANES), 0) < iota((LANES, LANES), 1))
    within = jnp.dot(member_low, before, preferred_element_type=F32)
    totals = jnp.dot(member_low, jnp.ones((LANES, LANES), BF16), preferred_element_type=F32)
    size = n * tall
    shift = tall.bit_length() - 1
    row, col = iota((size, size), 0), iota((size, size), 1)
    above = one_hot(((row >> shift) == (col >> shift)) & (col < row))
    ranks = within + jnp.dot(above, totals.astype(BF16), preferred_element_type=F32)
    ranks = ranks * member
    rank = jnp.zeros((tall, LANES), F32)
    for f in range(n):
        rank = rank + ranks[f * tall:(f + 1) * tall]
    rank = rank.astype(I32)

    def as_row(x):
        return jnp.concatenate([x[i:i + 1] for i in range(blocks)], axis=1)

    return as_row(fam), as_row(rank), as_row(rel)


def pack(n, piece, which, grp, unit_ref, fam_row, rank_row, note_ref, outs):
    rows, width = unit_ref.shape
    pos = (fam_row ^ grp) * piece + rank_row
    for d, out in zip(which, outs):
        select = one_hot(iota((piece, rows), 0) + d * piece == pos)
        got = jnp.dot(select, unit_ref[...], preferred_element_type=F32)
        note = note_ref[grp ^ d]
        note = jnp.concatenate([note, jnp.zeros((NOTE, width - note.shape[1]), F32)], axis=1)
        out[...] = jnp.concatenate([got, note], axis=0).astype(BF16)


def first_kernel(n, piece, family_rows, which, here_ref, route_ref, cluster_ref, emb_ref, *rest):
    fam_ref, rank_ref, note_ref, unit_ref = rest[:4]
    outs = rest[4:4 + len(which)]
    rows = emb_ref.shape[0]
    fam_row, rank_row, rel_row = places(n, family_rows, route_ref[...])
    fam_ref[...] = fam_row
    rank_ref[...] = rank_row
    mine = iota((n, rows), 0) == fam_row
    high, low = [jnp.where(mine, x, 0.0) for x in digits(rel_row)]
    at_rank = one_hot(iota((piece, rows), 0) == rank_row)
    slots = dot_nt(jnp.concatenate([high, low], axis=0).astype(BF16), at_rank)
    cluster = cluster_ref[...]
    counts = []
    for c in range(CLUSTERS - 1):
        total = jnp.sum(jnp.where(cluster <= c, 1.0, 0.0), axis=1, keepdims=True)
        counts += digits(jnp.broadcast_to(total, (1, piece)).astype(I32))
    counts = jnp.concatenate(counts, axis=0)
    spare = note_ref.shape[-1] - piece
    for f in range(n):
        note = jnp.concatenate([slots[f:f + 1], slots[n + f:n + f + 1], counts], axis=0)
        if spare:
            note = jnp.concatenate([note, jnp.zeros((NOTE, spare), F32)], axis=1)
        note_ref[f] = note

    @pl.loop(0, rows // 128)
    def _(i):
        at = pl.ds(pl.multiple_of(i * 128, 128), 128)
        x = emb_ref[at, :].astype(F32)
        total = jnp.sum(x * x, axis=1, keepdims=True)
        unit_ref[at, :] = (x * lax.rsqrt(total + 1e-06)).astype(BF16)

    pack(n, piece, which, here_ref[0], unit_ref, fam_row, rank_row, note_ref, outs)


def second_kernel(n, piece, which, here_ref, fam_ref, rank_ref, note_ref, unit_ref, *outs):
    pack(n, piece, which, here_ref[0], unit_ref, fam_ref[...], rank_ref[...], note_ref, outs)


def stage_kernel(n, nb, piece, lo, hi, here_ref, *rest):
    count = hi - lo
    home = rest[:nb]
    pieces = [rest[(1 + i) * nb:(2 + i) * nb] for i in range(count)]
    rest = rest[(1 + count) * nb + (4 if lo else 0):]
    out_ref, keys, best, key_kinds, query_kinds = rest
    grp, blk = here_ref[0], here_ref[1]
    width = keys.shape[-1]
    span = nb * piece
    wide = -(-piece // LANES) * LANES

    def note_of(ref):
        return ref[piece:, :wide].astype(F32)

    bounds = [jnp.zeros((1, piece), F32)] * (CLUSTERS - 1)
    for e in range(nb):
        note = note_of(home[e])[:, :piece]
        bounds = [
            b + note[2 + 2 * c:3 + 2 * c] * 64.0 + note[3 + 2 * c:4 + 2 * c]
            for c, b in enumerate(bounds)
        ]
    first = iota((8, piece), 0) == 0
    ones = jnp.where(iota((8, LANES), 0) == 0, 1.0, 0.0).astype(BF16)
    if not lo:
        best[...] = jnp.full(best.shape, -1.0, F32)
    for i in range(count):
        column = grp ^ (lo + i)
        for e in range(nb):
            ref = pieces[i][e]
            keys[column, blk ^ e] = ref[:piece]
            note = note_of(ref)[:, :piece]
            slots = note[0:1] * 64.0 + note[1:2]
            kinds = jnp.zeros((1, piece), F32)
            for bound in bounds:
                kinds = kinds + jnp.where(slots >= bound, 1.0, 0.0)
            if not e:
                query_kinds[column] = kinds
            key_kinds[column * nb + (blk ^ e)] = lax.dot_general(
                jnp.where(first, kinds, 0.0).astype(BF16),
                ones,
                (((0,), (0,)), ((), ())),
                preferred_element_type=F32,
            )

    def fold(query, key, causal):
        q = keys[query, blk]
        for half in range(2):
            rows = span // 2
            k = keys[key, half * nb // 2:(half + 1) * nb // 2].reshape(rows, width)
            scores = dot_nt(k, q)
            kinds = key_kinds[pl.ds(key * nb + half * nb // 2, nb // 2)].reshape(rows, LANES)
            parts = []
            for at in range(0, piece, LANES):
                w = min(LANES, piece - at)
                match = kinds[:, :w] == query_kinds[query][:, at:at + w]
                if causal:
                    early = iota((rows, w), 0) - iota((rows, w), 1) < blk * piece + (at - half * rows)
                    match = match & early
                part = jnp.where(match, scores[:, at:at + w], -1.0)
                parts.append(jnp.max(part.reshape(rows // 8, 8, w), axis=0))
            folded = jnp.concatenate(parts, axis=1) if len(parts) > 1 else parts[0]
            best[query] = jnp.maximum(best[query], folded)

    @pl.loop(lo, hi)
    def _(a):
        one = grp ^ a
        fold(one, one, True)

        @pl.loop(0, a)
        def _(b):
            two = grp ^ b
            fold(jnp.maximum(one, two), jnp.minimum(one, two), False)

    if hi == n:
        for f in range(n):
            out_ref[f] = jnp.max(best[f], axis=0, keepdims=True)
    else:
        out_ref[...] = jnp.zeros(out_ref.shape, F32)


def unpack_kernel(n, piece, fam_ref, rank_ref, score_ref, out_ref):
    x = jnp.concatenate([score_ref[f] for f in range(n)], axis=0)
    high = x.astype(BF16)
    rest = x - high.astype(F32)
    mid = rest.astype(BF16)
    low = (rest - mid.astype(F32)).astype(BF16)
    rows = fam_ref.shape[1]
    at_rank = one_hot(iota((piece, rows), 0) == rank_ref[...])
    got = jnp.dot(jnp.concatenate([high, mid, low], axis=0), at_rank, preferred_element_type=F32)
    value = got[:n] + got[n:2 * n] + got[2 * n:]
    value = jnp.where(iota((n, rows), 0) == fam_ref[...], value, 0.0)
    value = jnp.sum(value, axis=0, keepdims=True)
    for i in range(out_ref.shape[0]):
        out_ref[i:i + 1] = value[:, i * LANES:(i + 1) * LANES]


def shape(*dims, kind=F32):
    return jax.ShapeDtypeStruct(dims, kind)


def send(x, axis, by):
    return lax.ppermute(x, axis, [(i, i ^ by) for i in range(lax.axis_size(axis))])


def after(x, *deps):
    return pl.pallas_call(
        lambda *refs: None,
        out_shape=jax.ShapeDtypeStruct(x.shape, x.dtype),
        in_specs=[ANY] * (1 + len(deps)),
        out_specs=ANY,
        input_output_aliases={0: 0},
        cost_estimate=cost(0),
        name="after",
    )(x, *deps)


def limit(mib):
    return pltpu.CompilerParams(vmem_limit_bytes=mib * MIB)


def cost(flops):
    return pl.CostEstimate(flops=flops, bytes_accessed=0, transcendentals=0)


def on_device(embeddings, route, cluster):
    rows, width = embeddings.shape
    n, nb = lax.axis_size("grp"), lax.axis_size("blk")
    piece = rows // n
    half = n // 2
    grp, blk = lax.axis_index("grp"), lax.axis_index("blk")
    here = jnp.stack([grp, blk]).astype(I32)
    blocks = rows // LANES
    wide = -(-piece // LANES) * LANES
    one_piece = shape(piece + NOTE, width, kind=BF16)

    early = [half, half + 1, 0, 1]
    late = [d for d in range(n) if d not in early]
    fam, rank, note, unit, *packed = pl.pallas_call(
        functools.partial(first_kernel, n, piece, rows * nb, early),
        out_shape=[shape(1, rows, kind=I32)] * 2
        + [shape(n, NOTE, wide), shape(rows, width, kind=BF16)]
        + [one_piece] * len(early),
        in_specs=[SMEM, VMEM, VMEM, VMEM],
        out_specs=[VMEM] * (4 + len(early)),
        compiler_params=limit(16),
        name="first",
    )(here, route.reshape(blocks, LANES), cluster, embeddings)
    others = pl.pallas_call(
        functools.partial(second_kernel, n, piece, late),
        out_shape=[one_piece] * len(late),
        in_specs=[SMEM] + [VMEM] * 4,
        out_specs=[VMEM] * len(late),
        compiler_params=limit(16),
        cost_estimate=cost(8 * rows * rows * width),
        name="second",
    )(here, fam, rank, note, unit)
    sent = dict(zip(early + late, packed + list(others)))

    cuts = [0, half, half + 2, half + 3, n] if n == 8 else list(range(0, n + 1, 8))
    own, across, held = [None] * n, [None] * n, [None] * n

    own[0] = sent[0]
    across[0] = send(own[0], "blk", 2)
    for d in [half, half + 1] + list(range(1, half)) + list(range(half + 2, n)):
        dep = None if d in (1, half, half + 1) else across[0] if d < half else own[d - 2]
        own[d] = send(sent[d] if dep is None else after(sent[d], dep), "grp", d)
    state, tokens = [], []
    for lo, hi in zip(cuts, cuts[1:]):
        for d in range(lo, hi):
            x = own[d]
            across[d] = send(x, "blk", 2) if d else across[0]
            held[d] = [x, send(x, "blk", 1), across[d], send(across[d], "blk", 1)]
        kept = [
            shape(n, nb, piece, width, kind=BF16),
            shape(n, 8, piece),
            shape(n * nb, piece, LANES),
            shape(n, 1, piece),
        ]
        folds = sum(d + 1 for d in range(lo, hi))
        args = [here] + held[0] + [p for d in range(lo, hi) for p in held[d]] + list(state)
        token, *state = pl.pallas_call(
            functools.partial(stage_kernel, n, nb, piece, lo, hi),
            out_shape=[shape(n, 1, piece) if hi == n else shape(8, LANES)] + kept,
            in_specs=[SMEM] + [VMEM] * (len(args) - 1),
            out_specs=[VMEM] * 5,
            input_output_aliases={len(args) - 4 + i: 1 + i for i in range(4)} if lo else {},
            compiler_params=limit(12),
            cost_estimate=cost(folds * 2 * piece * piece * nb * width),
            name="stage",
        )(*args)
        tokens.append(token)

    home = lax.all_to_all(token, "grp", split_axis=0, concat_axis=0, tiled=True)
    out = pl.pallas_call(
        functools.partial(unpack_kernel, n, piece),
        out_shape=shape(blocks, LANES),
        in_specs=[VMEM] * 3,
        out_specs=VMEM,
        compiler_params=limit(16),
        name="unpack",
    )(fam, rank, home)
    return out.reshape(rows)


def solution(mesh):
    in_specs = (P(("grp", "blk"), None), P(("grp", "blk")), P("grp", "blk"))
    return jax.shard_map(
        on_device, mesh=mesh, in_specs=in_specs, out_specs=P(("grp", "blk")), check_vma=False
    )
```

```python
import functools

import jax
import jax.numpy as jnp
from jax import lax
from jax.experimental import pallas as pl
from jax.experimental.pallas import tpu as pltpu
from jax.sharding import PartitionSpec as P

BF16, F32, I32 = jnp.bfloat16, jnp.float32, jnp.int32
LANES = 128
CLUSTERS = 4
NOTE = 8
VMEM = pl.BlockSpec(memory_space=pltpu.VMEM)
SMEM = pl.BlockSpec(memory_space=pltpu.SMEM)
MIB = 1 << 20


def dot_nt(a, b):
    return lax.dot_general(a, b, (((1,), (1,)), ((), ())), preferred_element_type=F32)


def iota(shape, dim):
    return lax.broadcasted_iota(I32, shape, dim)


def one_hot(match):
    return jnp.where(match, 1.0, 0.0).astype(BF16)


def digits(x):
    return [(x >> 6).astype(F32), (x & 63).astype(F32)]


def places(n, family_rows, route):
    blocks = route.shape[0]
    fam = jnp.zeros_like(route)
    for f in range(1, n):
        fam = fam + jnp.where(route >= f * family_rows, 1, 0)
    rel = route - fam * family_rows
    pad = -blocks % 16
    tall = blocks + pad
    fam_pad = jnp.concatenate([fam, jnp.full((pad, LANES), -1, I32)], axis=0) if pad else fam
    member = jnp.concatenate([jnp.where(fam_pad == f, 1.0, 0.0) for f in range(n)], axis=0)
    member_low = member.astype(BF16)
    before = one_hot(iota((LANES, LANES), 0) < iota((LANES, LANES), 1))
    within = jnp.dot(member_low, before, preferred_element_type=F32)
    totals = jnp.dot(member_low, jnp.ones((LANES, LANES), BF16), preferred_element_type=F32)
    size = n * tall
    shift = tall.bit_length() - 1
    row, col = iota((size, size), 0), iota((size, size), 1)
    above = one_hot(((row >> shift) == (col >> shift)) & (col < row))
    ranks = within + jnp.dot(above, totals.astype(BF16), preferred_element_type=F32)
    ranks = ranks * member
    rank = jnp.zeros((tall, LANES), F32)
    for f in range(n):
        rank = rank + ranks[f * tall:(f + 1) * tall]
    rank = rank.astype(I32)

    def as_row(x):
        return jnp.concatenate([x[i:i + 1] for i in range(blocks)], axis=1)

    return as_row(fam), as_row(rank), as_row(rel)


def pack(n, piece, which, grp, unit_ref, fam_row, rank_row, note_ref, outs):
    rows, width = unit_ref.shape
    pos = (fam_row ^ grp) * piece + rank_row
    for d, out in zip(which, outs):
        select = one_hot(iota((piece, rows), 0) + d * piece == pos)
        got = jnp.dot(select, unit_ref[...], preferred_element_type=F32)
        note = note_ref[grp ^ d]
        note = jnp.concatenate([note, jnp.zeros((NOTE, width - note.shape[1]), F32)], axis=1)
        out[...] = jnp.concatenate([got, note], axis=0).astype(BF16)


def first_kernel(n, piece, family_rows, which, here_ref, route_ref, cluster_ref, emb_ref, *rest):
    fam_ref, rank_ref, note_ref, unit_ref = rest[:4]
    outs = rest[4:4 + len(which)]
    rows = emb_ref.shape[0]
    fam_row, rank_row, rel_row = places(n, family_rows, route_ref[...])
    fam_ref[...] = fam_row
    rank_ref[...] = rank_row
    mine = iota((n, rows), 0) == fam_row
    high, low = [jnp.where(mine, x, 0.0) for x in digits(rel_row)]
    at_rank = one_hot(iota((piece, rows), 0) == rank_row)
    slots = dot_nt(jnp.concatenate([high, low], axis=0).astype(BF16), at_rank)
    cluster = cluster_ref[...]
    counts = []
    for c in range(CLUSTERS - 1):
        total = jnp.sum(jnp.where(cluster <= c, 1.0, 0.0), axis=1, keepdims=True)
        counts += digits(jnp.broadcast_to(total, (1, piece)).astype(I32))
    counts = jnp.concatenate(counts, axis=0)
    spare = note_ref.shape[-1] - piece
    for f in range(n):
        note = jnp.concatenate([slots[f:f + 1], slots[n + f:n + f + 1], counts], axis=0)
        if spare:
            note = jnp.concatenate([note, jnp.zeros((NOTE, spare), F32)], axis=1)
        note_ref[f] = note

    @pl.loop(0, rows // 128)
    def _(i):
        at = pl.ds(pl.multiple_of(i * 128, 128), 128)
        x = emb_ref[at, :].astype(F32)
        total = jnp.sum(x * x, axis=1, keepdims=True)
        unit_ref[at, :] = (x * lax.rsqrt(total + 1e-06)).astype(BF16)

    pack(n, piece, which, here_ref[0], unit_ref, fam_row, rank_row, note_ref, outs)


def second_kernel(n, piece, which, here_ref, fam_ref, rank_ref, note_ref, unit_ref, *rest):
    *outs, token_ref = rest
    token_ref[...] = jnp.zeros(token_ref.shape, F32)
    pack(n, piece, which, here_ref[0], unit_ref, fam_ref[...], rank_ref[...], note_ref, outs)


def join_kernel(count, *refs):
    out_ref = refs[-1]
    for i in range(count):
        out_ref[i] = refs[i][...]


def stage_kernel(n, nb, piece, old, groups, here_ref, token_ref, *rest):
    new = [d for group in groups for d in group]
    pieces = [
        [rest[i * nb + e].at[j] for e in range(nb)]
        for i, group in enumerate(groups)
        for j in range(len(group))
    ]
    out_ref, keys, best, key_kinds, query_kinds, bounds_ref = rest[-6:]
    grp, blk = here_ref[0], here_ref[1]
    width = keys.shape[-1]
    span = nb * piece
    wide = -(-piece // LANES) * LANES

    def note_of(ref):
        return ref[piece:, :wide].astype(F32)

    if not old:
        bounds = [jnp.zeros((1, piece), F32)] * (CLUSTERS - 1)
        for ref in pieces[0]:
            note = note_of(ref)[:, :piece]
            bounds = [
                b + note[2 + 2 * c:3 + 2 * c] * 64.0 + note[3 + 2 * c:4 + 2 * c]
                for c, b in enumerate(bounds)
            ]
        for c, bound in enumerate(bounds):
            bounds_ref[c] = bound
    bounds = [bounds_ref[c] for c in range(CLUSTERS - 1)]
    first = iota((8, piece), 0) == 0
    ones = jnp.where(iota((8, LANES), 0) == 0, 1.0, 0.0).astype(BF16)
    if not old:
        best[...] = jnp.full(best.shape, -1.0, F32)
    for d, refs in zip(new, pieces):
        column = grp ^ d
        for e, ref in enumerate(refs):
            keys[column, blk ^ e] = ref[:piece]
            note = note_of(ref)[:, :piece]
            slots = note[0:1] * 64.0 + note[1:2]
            kinds = jnp.zeros((1, piece), F32)
            for bound in bounds:
                kinds = kinds + jnp.where(slots >= bound, 1.0, 0.0)
            if not e:
                query_kinds[column] = kinds
            key_kinds[column * nb + (blk ^ e)] = lax.dot_general(
                jnp.where(first, kinds, 0.0).astype(BF16),
                ones,
                (((0,), (0,)), ((), ())),
                preferred_element_type=F32,
            )

    def fold(query, key, causal):
        scores = dot_nt(keys[key].reshape(span, width), keys[query, blk])
        kinds = key_kinds[pl.ds(key * nb, nb)].reshape(span, LANES)
        parts = []
        for at in range(0, piece, LANES):
            w = min(LANES, piece - at)
            match = kinds[:, :w] == query_kinds[query][:, at:at + w]
            if causal:
                early = iota((span, w), 0) - iota((span, w), 1) < blk * piece + at
                match = match & early
            part = jnp.where(match, scores[:, at:at + w], -1.0)
            parts.append(jnp.max(part.reshape(span // 8, 8, w), axis=0))
        folded = jnp.concatenate(parts, axis=1) if len(parts) > 1 else parts[0]
        best[query] = jnp.maximum(best[query], folded)

    def pair(a, b):
        one, two = grp ^ a, grp ^ b
        fold(jnp.maximum(one, two), jnp.minimum(one, two), False)

    if n <= 8:
        for i, a in enumerate(new):
            fold(grp ^ a, grp ^ a, True)
            for b in old + new[:i]:
                pair(a, b)
    else:
        @pl.loop(len(old), len(old) + len(new))
        def _(a):
            fold(grp ^ a, grp ^ a, True)

            @pl.loop(0, a)
            def _(b):
                pair(a, b)

    if len(old) + len(new) == n:
        for f in range(n):
            out_ref[f] = jnp.max(best[f], axis=0, keepdims=True)


def unpack_kernel(n, piece, fam_ref, rank_ref, score_ref, out_ref):
    x = jnp.concatenate([score_ref[f] for f in range(n)], axis=0)
    high = x.astype(BF16)
    rest = x - high.astype(F32)
    mid = rest.astype(BF16)
    low = (rest - mid.astype(F32)).astype(BF16)
    rows = fam_ref.shape[1]
    at_rank = one_hot(iota((piece, rows), 0) == rank_ref[...])
    got = jnp.dot(jnp.concatenate([high, mid, low], axis=0), at_rank, preferred_element_type=F32)
    value = got[:n] + got[n:2 * n] + got[2 * n:]
    value = jnp.where(iota((n, rows), 0) == fam_ref[...], value, 0.0)
    value = jnp.sum(value, axis=0, keepdims=True)
    for i in range(out_ref.shape[0]):
        out_ref[i:i + 1] = value[:, i * LANES:(i + 1) * LANES]


def shape(*dims, kind=F32):
    return jax.ShapeDtypeStruct(dims, kind)


def send(x, axis, by):
    return lax.ppermute(x, axis, [(i, i ^ by) for i in range(lax.axis_size(axis))])


def limit(mib):
    return pltpu.CompilerParams(vmem_limit_bytes=mib * MIB)


def cost(flops):
    return pl.CostEstimate(flops=flops, bytes_accessed=0, transcendentals=0)


def on_device(embeddings, route, cluster):
    rows, width = embeddings.shape
    n, nb = lax.axis_size("grp"), lax.axis_size("blk")
    piece = rows // n
    half = n // 2
    grp, blk = lax.axis_index("grp"), lax.axis_index("blk")
    here = jnp.stack([grp, blk]).astype(I32)
    blocks = rows // LANES
    wide = -(-piece // LANES) * LANES
    one_piece = shape(piece + NOTE, width, kind=BF16)

    early = [half, 0, 1]
    late = [d for d in range(n) if d not in early]
    fam, rank, note, unit, *packed = pl.pallas_call(
        functools.partial(first_kernel, n, piece, rows * nb, early),
        out_shape=[shape(1, rows, kind=I32)] * 2
        + [shape(n, NOTE, wide), shape(rows, width, kind=BF16)]
        + [one_piece] * len(early),
        in_specs=[SMEM, VMEM, VMEM, VMEM],
        out_specs=[VMEM] * (4 + len(early)),
        compiler_params=limit(16),
        name="first",
    )(here, route.reshape(blocks, LANES), cluster, embeddings)
    *others, token = pl.pallas_call(
        functools.partial(second_kernel, n, piece, late),
        out_shape=[one_piece] * len(late) + [shape(8, LANES)],
        in_specs=[SMEM] + [VMEM] * 4,
        out_specs=[VMEM] * (len(late) + 1),
        compiler_params=limit(16),
        cost_estimate=cost(8 * rows * rows * width),
        name="second",
    )(here, fam, rank, note, unit)
    sent = dict(zip(early + late, packed + others))
    own, seen, state = {0: sent[0]}, [], []

    def to_columns(*ds):
        for d in ds:
            own[d] = send(sent[d], "grp", d)

    def join(ds, later=()):
        nonlocal token
        ins = [own[d] for d in ds]
        kept = [token, *later]
        token, *later, joined = pl.pallas_call(
            functools.partial(join_kernel, len(ins)),
            out_shape=[jax.ShapeDtypeStruct(x.shape, x.dtype) for x in kept]
            + [shape(len(ins), *one_piece.shape, kind=BF16)],
            in_specs=[VMEM] * (len(ins) + len(kept)),
            out_specs=[VMEM] * (len(kept) + 1),
            input_output_aliases={len(ins) + i: i for i in range(len(kept))},
            compiler_params=limit(4),
            cost_estimate=cost(0),
            name="join",
        )(*ins, *kept)
        return [joined, *later]

    def stage(*groups):
        nonlocal token, seen, state
        kept = [
            shape(n, nb, piece, width, kind=BF16),
            shape(n, 8, piece),
            shape(n * nb, piece, LANES),
            shape(n, 1, piece),
            shape(CLUSTERS - 1, 1, piece),
        ]
        args = [here, token]
        for _, mine, across in groups:
            args += [mine, send(mine, "blk", 1), across, send(across, "blk", 1)]
        args += list(state)
        ds = [list(group[0]) for group in groups]
        now = seen + sum(ds, [])
        outs = [shape(8, LANES)] + ([shape(n, 1, piece)] if len(now) == n else []) + kept
        alias = {1: 0}
        if seen:
            alias |= {len(args) - 5 + i: len(outs) - 5 + i for i in range(5)}
        folds = sum(range(len(seen) + 1, len(now) + 1))
        token, *state = pl.pallas_call(
            functools.partial(stage_kernel, n, nb, piece, seen, ds),
            out_shape=outs,
            in_specs=[SMEM] + [VMEM] * (len(args) - 1),
            out_specs=[VMEM] * len(outs),
            input_output_aliases=alias,
            compiler_params=limit(12),
            cost_estimate=cost(folds * 4 * piece * piece * nb * width),
            name="stage",
        )(*args)
        seen = now

    if n == 8:
        to_columns(4, 1)
        one = own[0].reshape(1, *one_piece.shape)
        one_across = send(one, "blk", 2)
        two, one_across, sent[5], sent[2], sent[3] = join(
            (1, 4), [one_across, sent[5], sent[2], sent[3]]
        )
        two_across = send(two, "blk", 2)
        to_columns(5, 2, 3)
        three, two, two_across, sent[6] = join((2, 5), [two, two_across, sent[6]])
        three_across = send(three, "blk", 2)
        to_columns(6)
        four, three, three_across, sent[7] = join((3, 6), [three, three_across, sent[7]])
        four_across = send(four, "blk", 2)
        to_columns(7)
        stage(((0,), one, one_across), ((1, 4), two, two_across), ((2, 5), three, three_across))
        five, four, four_across = join((7,), [four, four_across])
        five_across = send(five, "blk", 2)
        stage(((3, 6), four, four_across))
        stage(((7,), five, five_across))
    else:
        to_columns(*range(1, n))
        for lo in range(0, n, 8):
            ds = range(lo, lo + 8)
            (joined,) = join(ds)
            stage((ds, joined, send(joined, "blk", 2)))
    scores = state[0]

    home = lax.all_to_all(scores, "grp", split_axis=0, concat_axis=0, tiled=True)
    out = pl.pallas_call(
        functools.partial(unpack_kernel, n, piece),
        out_shape=shape(blocks, LANES),
        in_specs=[VMEM] * 3,
        out_specs=VMEM,
        compiler_params=limit(16),
        name="unpack",
    )(fam, rank, home)
    return out.reshape(rows)


def solution(mesh):
    in_specs = (P(("grp", "blk"), None), P(("grp", "blk")), P("grp", "blk"))
    return jax.shard_map(
        on_device, mesh=mesh, in_specs=in_specs, out_specs=P(("grp", "blk")), check_vma=False
    )
```

```python
import functools

import jax
import jax.numpy as jnp
from jax import lax
from jax.experimental import pallas as pl
from jax.experimental.pallas import tpu as pltpu
from jax.sharding import PartitionSpec as P

BF16, F32, I32 = jnp.bfloat16, jnp.float32, jnp.int32
LANES = 128
CLUSTERS = 4
NOTE = 8
VMEM = pl.BlockSpec(memory_space=pltpu.VMEM)
SMEM = pl.BlockSpec(memory_space=pltpu.SMEM)
MIB = 1 << 20


def dot_nt(a, b):
    return lax.dot_general(a, b, (((1,), (1,)), ((), ())), preferred_element_type=F32)


def iota(shape, dim):
    return lax.broadcasted_iota(I32, shape, dim)


def one_hot(match):
    return jnp.where(match, 1.0, 0.0).astype(BF16)


def digits(x):
    return [(x >> 6).astype(F32), (x & 63).astype(F32)]


def places(n, family_rows, route):
    blocks = route.shape[0]
    fam = jnp.zeros_like(route)
    for f in range(1, n):
        fam = fam + jnp.where(route >= f * family_rows, 1, 0)
    rel = route - fam * family_rows
    pad = -blocks % 16
    tall = blocks + pad
    fam_pad = jnp.concatenate([fam, jnp.full((pad, LANES), -1, I32)], axis=0) if pad else fam
    member = jnp.concatenate([jnp.where(fam_pad == f, 1.0, 0.0) for f in range(n)], axis=0)
    member_low = member.astype(BF16)
    before = one_hot(iota((LANES, LANES), 0) < iota((LANES, LANES), 1))
    within = jnp.dot(member_low, before, preferred_element_type=F32)
    totals = jnp.dot(member_low, jnp.ones((LANES, LANES), BF16), preferred_element_type=F32)
    size = n * tall
    shift = tall.bit_length() - 1
    row, col = iota((size, size), 0), iota((size, size), 1)
    above = one_hot(((row >> shift) == (col >> shift)) & (col < row))
    ranks = within + jnp.dot(above, totals.astype(BF16), preferred_element_type=F32)
    ranks = ranks * member
    rank = jnp.zeros((tall, LANES), F32)
    for f in range(n):
        rank = rank + ranks[f * tall:(f + 1) * tall]
    rank = rank.astype(I32)

    def as_row(x):
        return jnp.concatenate([x[i:i + 1] for i in range(blocks)], axis=1)

    return as_row(fam), as_row(rank), as_row(rel)


def pack(n, piece, which, grp, unit_ref, fam_row, rank_row, note_ref, outs):
    rows, width = unit_ref.shape
    pos = (fam_row ^ grp) * piece + rank_row
    for d, out in zip(which, outs):
        select = one_hot(iota((piece, rows), 0) + d * piece == pos)
        got = jnp.dot(select, unit_ref[...], preferred_element_type=F32)
        note = note_ref[grp ^ d]
        note = jnp.concatenate([note, jnp.zeros((NOTE, width - note.shape[1]), F32)], axis=1)
        out[:piece + NOTE] = jnp.concatenate([got, note], axis=0).astype(BF16)
        if out.shape[0] > piece + NOTE:
            out[piece + NOTE:] = jnp.zeros((out.shape[0] - piece - NOTE, width), BF16)


def first_kernel(n, piece, family_rows, which, here_ref, route_ref, cluster_ref, emb_ref, *rest):
    fam_ref, rank_ref, note_ref, unit_ref = rest[:4]
    outs = rest[4:4 + len(which)]
    rows = emb_ref.shape[0]
    fam_row, rank_row, rel_row = places(n, family_rows, route_ref[...])
    fam_ref[...] = fam_row
    rank_ref[...] = rank_row
    mine = iota((n, rows), 0) == fam_row
    high, low = [jnp.where(mine, x, 0.0) for x in digits(rel_row)]
    at_rank = one_hot(iota((piece, rows), 0) == rank_row)
    slots = dot_nt(jnp.concatenate([high, low], axis=0).astype(BF16), at_rank)
    cluster = cluster_ref[...]
    counts = []
    for c in range(CLUSTERS - 1):
        total = jnp.sum(jnp.where(cluster <= c, 1.0, 0.0), axis=1, keepdims=True)
        counts += digits(jnp.broadcast_to(total, (1, piece)).astype(I32))
    counts = jnp.concatenate(counts, axis=0)
    spare = note_ref.shape[-1] - piece
    for f in range(n):
        note = jnp.concatenate([slots[f:f + 1], slots[n + f:n + f + 1], counts], axis=0)
        if spare:
            note = jnp.concatenate([note, jnp.zeros((NOTE, spare), F32)], axis=1)
        note_ref[f] = note

    @pl.loop(0, rows // 128)
    def _(i):
        at = pl.ds(pl.multiple_of(i * 128, 128), 128)
        x = emb_ref[at, :].astype(F32)
        total = jnp.sum(x * x, axis=1, keepdims=True)
        unit_ref[at, :] = (x * lax.rsqrt(total + 1e-06)).astype(BF16)

    pack(n, piece, which, here_ref[0], unit_ref, fam_row, rank_row, note_ref, outs)


def second_kernel(n, piece, which, here_ref, fam_ref, rank_ref, note_ref, unit_ref, *rest):
    *outs, token_ref = rest
    token_ref[...] = jnp.zeros(token_ref.shape, F32)
    pack(n, piece, which, here_ref[0], unit_ref, fam_ref[...], rank_ref[...], note_ref, outs)


def join_kernel(count, *refs):
    out_ref = refs[-1]
    for i in range(count):
        out_ref[i] = refs[i][:out_ref.shape[1]]


def stage_kernel(n, nb, piece, old, groups, here_ref, token_ref, *rest):
    new = [d for group in groups for d in group]
    pieces = [
        [rest[i * nb + e].at[j] for e in range(nb)]
        for i, group in enumerate(groups)
        for j in range(len(group))
    ]
    out_ref, keys, best, key_kinds, query_kinds, bounds_ref = rest[-6:]
    grp, blk = here_ref[0], here_ref[1]
    width = keys.shape[-1]
    span = nb * piece
    wide = -(-piece // LANES) * LANES

    def note_of(ref):
        return ref[piece:, :wide].astype(F32)

    if not old:
        bounds = [jnp.zeros((1, piece), F32)] * (CLUSTERS - 1)
        for ref in pieces[0]:
            note = note_of(ref)[:, :piece]
            bounds = [
                b + note[2 + 2 * c:3 + 2 * c] * 64.0 + note[3 + 2 * c:4 + 2 * c]
                for c, b in enumerate(bounds)
            ]
        for c, bound in enumerate(bounds):
            bounds_ref[c] = bound
    bounds = [bounds_ref[c] for c in range(CLUSTERS - 1)]
    first = iota((8, piece), 0) == 0
    ones = jnp.where(iota((8, LANES), 0) == 0, 1.0, 0.0).astype(BF16)
    if not old:
        best[...] = jnp.full(best.shape, -1.0, F32)
    for d, refs in zip(new, pieces):
        column = grp ^ d
        for e, ref in enumerate(refs):
            keys[column, blk ^ e] = ref[:piece]
            note = note_of(ref)[:, :piece]
            slots = note[0:1] * 64.0 + note[1:2]
            kinds = jnp.zeros((1, piece), F32)
            for bound in bounds:
                kinds = kinds + jnp.where(slots >= bound, 1.0, 0.0)
            if not e:
                query_kinds[column] = kinds
            key_kinds[column * nb + (blk ^ e)] = lax.dot_general(
                jnp.where(first, kinds, 0.0).astype(BF16),
                ones,
                (((0,), (0,)), ((), ())),
                preferred_element_type=F32,
            )

    def fold(query, key, causal):
        scores = dot_nt(keys[key].reshape(span, width), keys[query, blk])
        kinds = key_kinds[pl.ds(key * nb, nb)].reshape(span, LANES)
        parts = []
        for at in range(0, piece, LANES):
            w = min(LANES, piece - at)
            match = kinds[:, :w] == query_kinds[query][:, at:at + w]
            if causal:
                early = iota((span, w), 0) - iota((span, w), 1) < blk * piece + at
                match = match & early
            part = jnp.where(match, scores[:, at:at + w], -1.0)
            parts.append(jnp.max(part.reshape(span // 8, 8, w), axis=0))
        folded = jnp.concatenate(parts, axis=1) if len(parts) > 1 else parts[0]
        best[query] = jnp.maximum(best[query], folded)

    def pair(a, b):
        one, two = grp ^ a, grp ^ b
        fold(jnp.maximum(one, two), jnp.minimum(one, two), False)

    if n <= 8:
        for i, a in enumerate(new):
            fold(grp ^ a, grp ^ a, True)
            for b in old + new[:i]:
                pair(a, b)
    else:
        @pl.loop(len(old), len(old) + len(new))
        def _(a):
            fold(grp ^ a, grp ^ a, True)

            @pl.loop(0, a)
            def _(b):
                pair(a, b)

    if len(old) + len(new) == n:
        for f in range(n):
            out_ref[f] = jnp.max(best[f], axis=0, keepdims=True)


def unpack_kernel(n, piece, fam_ref, rank_ref, score_ref, out_ref):
    x = jnp.concatenate([score_ref[f] for f in range(n)], axis=0)
    high = x.astype(BF16)
    rest = x - high.astype(F32)
    mid = rest.astype(BF16)
    low = (rest - mid.astype(F32)).astype(BF16)
    rows = fam_ref.shape[1]
    at_rank = one_hot(iota((piece, rows), 0) == rank_ref[...])
    got = jnp.dot(jnp.concatenate([high, mid, low], axis=0), at_rank, preferred_element_type=F32)
    value = got[:n] + got[n:2 * n] + got[2 * n:]
    value = jnp.where(iota((n, rows), 0) == fam_ref[...], value, 0.0)
    value = jnp.sum(value, axis=0, keepdims=True)
    for i in range(out_ref.shape[0]):
        out_ref[i:i + 1] = value[:, i * LANES:(i + 1) * LANES]


def shape(*dims, kind=F32):
    return jax.ShapeDtypeStruct(dims, kind)


def send(x, axis, by):
    return lax.ppermute(x, axis, [(i, i ^ by) for i in range(lax.axis_size(axis))])


def limit(mib):
    return pltpu.CompilerParams(vmem_limit_bytes=mib * MIB)


def cost(flops):
    return pl.CostEstimate(flops=flops, bytes_accessed=0, transcendentals=0)


def on_device(embeddings, route, cluster):
    rows, width = embeddings.shape
    n, nb = lax.axis_size("grp"), lax.axis_size("blk")
    piece = rows // n
    half = n // 2
    grp, blk = lax.axis_index("grp"), lax.axis_index("blk")
    here = jnp.stack([grp, blk]).astype(I32)
    blocks = rows // LANES
    wide = -(-piece // LANES) * LANES
    one_piece = shape(piece + NOTE, width, kind=BF16)
    longer = shape(piece + 2 * NOTE, width, kind=BF16)
    kind_of = {d: longer if n == 8 and d in (4, 6) else one_piece for d in range(n)}

    early = [half, 0, 1]
    late = [d for d in range(n) if d not in early]
    fam, rank, note, unit, *packed = pl.pallas_call(
        functools.partial(first_kernel, n, piece, rows * nb, early),
        out_shape=[shape(1, rows, kind=I32)] * 2
        + [shape(n, NOTE, wide), shape(rows, width, kind=BF16)]
        + [kind_of[d] for d in early],
        in_specs=[SMEM, VMEM, VMEM, VMEM],
        out_specs=[VMEM] * (4 + len(early)),
        compiler_params=limit(16),
        name="first",
    )(here, route.reshape(blocks, LANES), cluster, embeddings)
    *others, token = pl.pallas_call(
        functools.partial(second_kernel, n, piece, late),
        out_shape=[kind_of[d] for d in late] + [shape(8, LANES)],
        in_specs=[SMEM] + [VMEM] * 4,
        out_specs=[VMEM] * (len(late) + 1),
        compiler_params=limit(16),
        cost_estimate=cost(8 * rows * rows * width),
        name="second",
    )(here, fam, rank, note, unit)
    sent = dict(zip(early + late, packed + others))
    own, seen, state = {0: sent[0]}, [], []

    def to_columns(*ds):
        for d in ds:
            own[d] = send(sent[d], "grp", d)

    def join(ds, later=()):
        nonlocal token
        ins = [own[d] for d in ds]
        kept = [token, *later]
        joined = [shape(len(ins), *one_piece.shape, kind=BF16)] if ins else []
        token, *rest = pl.pallas_call(
            functools.partial(join_kernel, len(ins)),
            out_shape=[jax.ShapeDtypeStruct(x.shape, x.dtype) for x in kept] + joined,
            in_specs=[VMEM] * (len(ins) + len(kept)),
            out_specs=[VMEM] * (len(kept) + len(joined)),
            input_output_aliases={len(ins) + i: i for i in range(len(kept))},
            compiler_params=limit(4),
            cost_estimate=cost(0),
            name="join",
        )(*ins, *kept)
        return rest[len(later):] + rest[:len(later)]

    def stage(*groups):
        nonlocal token, seen, state
        kept = [
            shape(n, nb, piece, width, kind=BF16),
            shape(n, 8, piece),
            shape(n * nb, piece, LANES),
            shape(n, 1, piece),
            shape(CLUSTERS - 1, 1, piece),
        ]
        args = [here, token]
        for _, *four in groups:
            args += four
        args += list(state)
        ds = [list(group[0]) for group in groups]
        now = seen + sum(ds, [])
        outs = [shape(8, LANES)] + ([shape(n, 1, piece)] if len(now) == n else []) + kept
        alias = {1: 0}
        if seen:
            alias |= {len(args) - 5 + i: len(outs) - 5 + i for i in range(5)}
        folds = sum(range(len(seen) + 1, len(now) + 1))
        token, *state = pl.pallas_call(
            functools.partial(stage_kernel, n, nb, piece, seen, ds),
            out_shape=outs,
            in_specs=[SMEM] + [VMEM] * (len(args) - 1),
            out_specs=[VMEM] * len(outs),
            input_output_aliases=alias,
            compiler_params=limit(12),
            cost_estimate=cost(folds * 4 * piece * piece * nb * width),
            name="stage",
        )(*args)
        seen = now

    if n == 8:
        to_columns(4, 1)
        m0 = own[0].reshape(1, *one_piece.shape)
        y0, c0 = send(m0, "blk", 2), send(m0, "blk", 1)
        m1, y0, c0, sent[5], sent[2] = join((4, 1), [y0, c0, sent[5], sent[2]])
        to_columns(5, 2)
        y1, c1, x0 = send(m1, "blk", 2), send(m1, "blk", 1), send(y0, "blk", 1)
        m2, y1, c1, x0, sent[6], sent[3] = join((5, 2), [y1, c1, x0, sent[6], sent[3]])
        to_columns(6, 3)
        y2, c2, x1 = send(m2, "blk", 2), send(m2, "blk", 1), send(y1, "blk", 1)
        m3, y2, c2, x1, sent[7] = join((6, 3), [y2, c2, x1, sent[7]])
        to_columns(7)
        y3, c3, x2 = send(m3, "blk", 2), send(m3, "blk", 1), send(y2, "blk", 1)
        stage(((0,), m0, c0, y0, x0), ((4, 1), m1, c1, y1, x1), ((5, 2), m2, c2, y2, x2))
        m4, y3, c3 = join((7,), [y3, c3])
        y4, c4, x3 = send(m4, "blk", 2), send(m4, "blk", 1), send(y3, "blk", 1)
        stage(((6, 3), m3, c3, y3, x3))
        (y4,) = join((), [y4])
        stage(((7,), m4, c4, y4, send(y4, "blk", 1)))
    else:
        to_columns(*range(1, n))
        for lo in range(0, n, 8):
            ds = range(lo, lo + 8)
            (m,) = join(ds)
            y = send(m, "blk", 2)
            stage((ds, m, send(m, "blk", 1), y, send(y, "blk", 1)))
    scores = state[0]

    home = lax.all_to_all(scores, "grp", split_axis=0, concat_axis=0, tiled=True)
    out = pl.pallas_call(
        functools.partial(unpack_kernel, n, piece),
        out_shape=shape(blocks, LANES),
        in_specs=[VMEM] * 3,
        out_specs=VMEM,
        compiler_params=limit(16),
        name="unpack",
    )(fam, rank, home)
    return out.reshape(rows)


def solution(mesh):
    in_specs = (P(("grp", "blk"), None), P(("grp", "blk")), P("grp", "blk"))
    return jax.shard_map(
        on_device, mesh=mesh, in_specs=in_specs, out_specs=P(("grp", "blk")), check_vma=False
    )
```

```python
import functools

import jax
import jax.numpy as jnp
from jax import lax
from jax.experimental import pallas as pl
from jax.experimental.pallas import tpu as pltpu
from jax.sharding import PartitionSpec as P

BF16, F32, I32 = jnp.bfloat16, jnp.float32, jnp.int32
LANES = 128
CLUSTERS = 4
NOTE = 8
VMEM = pl.BlockSpec(memory_space=pltpu.VMEM)
SMEM = pl.BlockSpec(memory_space=pltpu.SMEM)
MIB = 1 << 20


def dot_nt(a, b):
    return lax.dot_general(a, b, (((1,), (1,)), ((), ())), preferred_element_type=F32)


def iota(shape, dim):
    return lax.broadcasted_iota(I32, shape, dim)


def one_hot(match):
    return jnp.where(match, 1.0, 0.0).astype(BF16)


def digits(x):
    return [(x >> 6).astype(F32), (x & 63).astype(F32)]


def places(n, family_rows, route):
    blocks = route.shape[0]
    fam = jnp.zeros_like(route)
    for f in range(1, n):
        fam = fam + jnp.where(route >= f * family_rows, 1, 0)
    rel = route - fam * family_rows
    pad = -blocks % 16
    tall = blocks + pad
    fam_pad = jnp.concatenate([fam, jnp.full((pad, LANES), -1, I32)], axis=0) if pad else fam
    member = jnp.concatenate([jnp.where(fam_pad == f, 1.0, 0.0) for f in range(n)], axis=0)
    member_low = member.astype(BF16)
    before = one_hot(iota((LANES, LANES), 0) < iota((LANES, LANES), 1))
    within = jnp.dot(member_low, before, preferred_element_type=F32)
    totals = jnp.dot(member_low, jnp.ones((LANES, LANES), BF16), preferred_element_type=F32)
    size = n * tall
    shift = tall.bit_length() - 1
    row, col = iota((size, size), 0), iota((size, size), 1)
    above = one_hot(((row >> shift) == (col >> shift)) & (col < row))
    ranks = within + jnp.dot(above, totals.astype(BF16), preferred_element_type=F32)
    ranks = ranks * member
    rank = jnp.zeros((tall, LANES), F32)
    for f in range(n):
        rank = rank + ranks[f * tall:(f + 1) * tall]
    rank = rank.astype(I32)

    def as_row(x):
        return jnp.concatenate([x[i:i + 1] for i in range(blocks)], axis=1)

    return as_row(fam), as_row(rank), as_row(rel)


def pack(n, piece, which, grp, unit_ref, fam_row, rank_row, note_ref, outs):
    rows, width = unit_ref.shape
    pos = (fam_row ^ grp) * piece + rank_row
    for d, out in zip(which, outs):
        select = one_hot(iota((piece, rows), 0) + d * piece == pos)
        got = jnp.dot(select, unit_ref[...], preferred_element_type=F32)
        note = note_ref[grp ^ d]
        note = jnp.concatenate([note, jnp.zeros((NOTE, width - note.shape[1]), F32)], axis=1)
        out[:piece + NOTE] = jnp.concatenate([got, note], axis=0).astype(BF16)
        if out.shape[0] > piece + NOTE:
            out[piece + NOTE:] = jnp.zeros((out.shape[0] - piece - NOTE, width), BF16)


def first_kernel(n, piece, family_rows, which, here_ref, route_ref, cluster_ref, emb_ref, *rest):
    fam_ref, rank_ref, note_ref, unit_ref = rest[:4]
    outs = rest[4:4 + len(which)]
    rows = emb_ref.shape[0]
    fam_row, rank_row, rel_row = places(n, family_rows, route_ref[...])
    fam_ref[...] = fam_row
    rank_ref[...] = rank_row
    mine = iota((n, rows), 0) == fam_row
    high, low = [jnp.where(mine, x, 0.0) for x in digits(rel_row)]
    at_rank = one_hot(iota((piece, rows), 0) == rank_row)
    slots = dot_nt(jnp.concatenate([high, low], axis=0).astype(BF16), at_rank)
    cluster = cluster_ref[...]
    counts = []
    for c in range(CLUSTERS - 1):
        total = jnp.sum(jnp.where(cluster <= c, 1.0, 0.0), axis=1, keepdims=True)
        counts += digits(jnp.broadcast_to(total, (1, piece)).astype(I32))
    counts = jnp.concatenate(counts, axis=0)
    spare = note_ref.shape[-1] - piece
    for f in range(n):
        note = jnp.concatenate([slots[f:f + 1], slots[n + f:n + f + 1], counts], axis=0)
        if spare:
            note = jnp.concatenate([note, jnp.zeros((NOTE, spare), F32)], axis=1)
        note_ref[f] = note

    @pl.loop(0, rows // 128)
    def _(i):
        at = pl.ds(pl.multiple_of(i * 128, 128), 128)
        x = emb_ref[at, :].astype(F32)
        total = jnp.sum(x * x, axis=1, keepdims=True)
        unit_ref[at, :] = (x * lax.rsqrt(total + 1e-06)).astype(BF16)

    pack(n, piece, which, here_ref[0], unit_ref, fam_row, rank_row, note_ref, outs)


def second_kernel(n, piece, which, here_ref, fam_ref, rank_ref, note_ref, unit_ref, *rest):
    *outs, token_ref = rest
    token_ref[...] = jnp.zeros(token_ref.shape, F32)
    pack(n, piece, which, here_ref[0], unit_ref, fam_ref[...], rank_ref[...], note_ref, outs)


def join_kernel(count, *refs):
    out_ref = refs[-1]
    for i in range(count):
        out_ref[i] = refs[i][:out_ref.shape[1]]


def stage_kernel(n, nb, piece, old, groups, here_ref, token_ref, *rest):
    new = [d for group in groups for d in group]
    pieces = [
        [rest[i * nb + e].at[j] for e in range(nb)]
        for i, group in enumerate(groups)
        for j in range(len(group))
    ]
    out_ref, keys, best, key_kinds, query_kinds, bounds_ref = rest[-6:]
    grp, blk = here_ref[0], here_ref[1]
    width = keys.shape[-1]
    span = nb * piece
    wide = -(-piece // LANES) * LANES

    def note_of(ref):
        return ref[piece:, :wide].astype(F32)

    if not old:
        bounds = [jnp.zeros((1, piece), F32)] * (CLUSTERS - 1)
        for ref in pieces[0]:
            note = note_of(ref)[:, :piece]
            bounds = [
                b + note[2 + 2 * c:3 + 2 * c] * 64.0 + note[3 + 2 * c:4 + 2 * c]
                for c, b in enumerate(bounds)
            ]
        for c, bound in enumerate(bounds):
            bounds_ref[c] = bound
    bounds = [bounds_ref[c] for c in range(CLUSTERS - 1)]
    first = iota((8, piece), 0) == 0
    ones = jnp.where(iota((8, LANES), 0) == 0, 1.0, 0.0).astype(BF16)
    if not old:
        best[...] = jnp.full(best.shape, -1.0, F32)
    for d, refs in zip(new, pieces):
        column = grp ^ d
        for e, ref in enumerate(refs):
            keys[column, blk ^ e] = ref[:piece]
            note = note_of(ref)[:, :piece]
            slots = note[0:1] * 64.0 + note[1:2]
            kinds = jnp.zeros((1, piece), F32)
            for bound in bounds:
                kinds = kinds + jnp.where(slots >= bound, 1.0, 0.0)
            if not e:
                query_kinds[column] = kinds
            key_kinds[column * nb + (blk ^ e)] = lax.dot_general(
                jnp.where(first, kinds, 0.0).astype(BF16),
                ones,
                (((0,), (0,)), ((), ())),
                preferred_element_type=F32,
            )

    def fold(query, key, causal):
        scores = dot_nt(keys[key].reshape(span, width), keys[query, blk])
        kinds = key_kinds[pl.ds(key * nb, nb)].reshape(span, LANES)
        parts = []
        for at in range(0, piece, LANES):
            w = min(LANES, piece - at)
            match = kinds[:, :w] == query_kinds[query][:, at:at + w]
            if causal:
                early = iota((span, w), 0) - iota((span, w), 1) < blk * piece + at
                match = match & early
            part = jnp.where(match, scores[:, at:at + w], -1.0)
            parts.append(jnp.max(part.reshape(span // 8, 8, w), axis=0))
        folded = jnp.concatenate(parts, axis=1) if len(parts) > 1 else parts[0]
        best[query] = jnp.maximum(best[query], folded)

    def pair(a, b):
        one, two = grp ^ a, grp ^ b
        fold(jnp.maximum(one, two), jnp.minimum(one, two), False)

    if n <= 8:
        for i, a in enumerate(new):
            fold(grp ^ a, grp ^ a, True)
            for b in old + new[:i]:
                pair(a, b)
    else:
        @pl.loop(len(old), len(old) + len(new))
        def _(a):
            fold(grp ^ a, grp ^ a, True)

            @pl.loop(0, a)
            def _(b):
                pair(a, b)

    if len(old) + len(new) == n:
        for f in range(n):
            out_ref[f] = jnp.max(best[f], axis=0, keepdims=True)


def unpack_kernel(n, piece, fam_ref, rank_ref, score_ref, out_ref):
    x = jnp.concatenate([score_ref[f] for f in range(n)], axis=0)
    high = x.astype(BF16)
    rest = x - high.astype(F32)
    mid = rest.astype(BF16)
    low = (rest - mid.astype(F32)).astype(BF16)
    rows = fam_ref.shape[1]
    at_rank = one_hot(iota((piece, rows), 0) == rank_ref[...])
    got = jnp.dot(jnp.concatenate([high, mid, low], axis=0), at_rank, preferred_element_type=F32)
    value = got[:n] + got[n:2 * n] + got[2 * n:]
    value = jnp.where(iota((n, rows), 0) == fam_ref[...], value, 0.0)
    value = jnp.sum(value, axis=0, keepdims=True)
    for i in range(out_ref.shape[0]):
        out_ref[i:i + 1] = value[:, i * LANES:(i + 1) * LANES]


def shape(*dims, kind=F32):
    return jax.ShapeDtypeStruct(dims, kind)


def send(x, axis, by):
    return lax.ppermute(x, axis, [(i, i ^ by) for i in range(lax.axis_size(axis))])


def limit(mib):
    return pltpu.CompilerParams(vmem_limit_bytes=mib * MIB)


def cost(flops):
    return pl.CostEstimate(flops=flops, bytes_accessed=0, transcendentals=0)


def on_device(embeddings, route, cluster):
    rows, width = embeddings.shape
    n, nb = lax.axis_size("grp"), lax.axis_size("blk")
    piece = rows // n
    half = n // 2
    grp, blk = lax.axis_index("grp"), lax.axis_index("blk")
    here = jnp.stack([grp, blk]).astype(I32)
    blocks = rows // LANES
    wide = -(-piece // LANES) * LANES
    one_piece = shape(piece + NOTE, width, kind=BF16)
    longer = shape(piece + 2 * NOTE, width, kind=BF16)
    kind_of = {d: longer if n == 8 and d in (2, 4, 6) else one_piece for d in range(n)}

    early = [half, 2]
    late = [d for d in range(n) if d not in early]
    fam, rank, note, unit, *packed = pl.pallas_call(
        functools.partial(first_kernel, n, piece, rows * nb, early),
        out_shape=[shape(1, rows, kind=I32)] * 2
        + [shape(n, NOTE, wide), shape(rows, width, kind=BF16)]
        + [kind_of[d] for d in early],
        in_specs=[SMEM, VMEM, VMEM, VMEM],
        out_specs=[VMEM] * (4 + len(early)),
        compiler_params=limit(16),
        name="first",
    )(here, route.reshape(blocks, LANES), cluster, embeddings)
    *others, token = pl.pallas_call(
        functools.partial(second_kernel, n, piece, late),
        out_shape=[kind_of[d] for d in late] + [shape(8, LANES)],
        in_specs=[SMEM] + [VMEM] * 4,
        out_specs=[VMEM] * (len(late) + 1),
        compiler_params=limit(16),
        cost_estimate=cost(8 * rows * rows * width),
        name="second",
    )(here, fam, rank, note, unit)
    sent = dict(zip(early + late, packed + others))
    own, seen, state = {0: sent[0]}, [], []

    def to_columns(*ds):
        for d in ds:
            own[d] = send(sent[d], "grp", d)

    def join(ds, later=()):
        nonlocal token
        ins = [own[d] for d in ds]
        kept = [token, *later]
        joined = [shape(len(ins), *one_piece.shape, kind=BF16)] if ins else []
        token, *rest = pl.pallas_call(
            functools.partial(join_kernel, len(ins)),
            out_shape=[jax.ShapeDtypeStruct(x.shape, x.dtype) for x in kept] + joined,
            in_specs=[VMEM] * (len(ins) + len(kept)),
            out_specs=[VMEM] * (len(kept) + len(joined)),
            input_output_aliases={len(ins) + i: i for i in range(len(kept))},
            compiler_params=limit(4),
            cost_estimate=cost(0),
            name="join",
        )(*ins, *kept)
        return rest[len(later):] + rest[:len(later)]

    def stage(*groups):
        nonlocal token, seen, state
        kept = [
            shape(n, nb, piece, width, kind=BF16),
            shape(n, 8, piece),
            shape(n * nb, piece, LANES),
            shape(n, 1, piece),
            shape(CLUSTERS - 1, 1, piece),
        ]
        args = [here, token]
        for _, *four in groups:
            args += four
        args += list(state)
        ds = [list(group[0]) for group in groups]
        now = seen + sum(ds, [])
        outs = [shape(8, LANES)] + ([shape(n, 1, piece)] if len(now) == n else []) + kept
        alias = {1: 0}
        if seen:
            alias |= {len(args) - 5 + i: len(outs) - 5 + i for i in range(5)}
        folds = sum(range(len(seen) + 1, len(now) + 1))
        token, *state = pl.pallas_call(
            functools.partial(stage_kernel, n, nb, piece, seen, ds),
            out_shape=outs,
            in_specs=[SMEM] + [VMEM] * (len(args) - 1),
            out_specs=[VMEM] * len(outs),
            input_output_aliases=alias,
            compiler_params=limit(12),
            cost_estimate=cost(folds * 4 * piece * piece * nb * width),
            name="stage",
        )(*args)
        seen = now

    if n == 8:
        to_columns(4, 2)
        m0 = own[0].reshape(1, *one_piece.shape)
        y0, c0 = send(m0, "blk", 2), send(m0, "blk", 1)
        m1, y0, c0, sent[5], sent[3] = join((4, 2), [y0, c0, sent[5], sent[3]])
        to_columns(5, 3)
        y1, c1, x0 = send(m1, "blk", 2), send(m1, "blk", 1), send(y0, "blk", 1)
        m2, y1, c1, x0, sent[6], sent[1] = join((5, 3), [y1, c1, x0, sent[6], sent[1]])
        to_columns(6, 1)
        y2, c2, x1 = send(m2, "blk", 2), send(m2, "blk", 1), send(y1, "blk", 1)
        m3, y2, c2, x1, sent[7] = join((6, 1), [y2, c2, x1, sent[7]])
        to_columns(7)
        y3, c3, x2 = send(m3, "blk", 2), send(m3, "blk", 1), send(y2, "blk", 1)
        stage(((0,), m0, c0, y0, x0), ((4, 2), m1, c1, y1, x1), ((5, 3), m2, c2, y2, x2))
        m4, y3, c3 = join((7,), [y3, c3])
        y4, c4, x3 = send(m4, "blk", 2), send(m4, "blk", 1), send(y3, "blk", 1)
        stage(((6, 1), m3, c3, y3, x3))
        (y4,) = join((), [y4])
        stage(((7,), m4, c4, y4, send(y4, "blk", 1)))
    else:
        to_columns(*range(1, n))
        for lo in range(0, n, 8):
            ds = range(lo, lo + 8)
            (m,) = join(ds)
            y = send(m, "blk", 2)
            stage((ds, m, send(m, "blk", 1), y, send(y, "blk", 1)))
    scores = state[0]

    home = lax.all_to_all(scores, "grp", split_axis=0, concat_axis=0, tiled=True)
    out = pl.pallas_call(
        functools.partial(unpack_kernel, n, piece),
        out_shape=shape(blocks, LANES),
        in_specs=[VMEM] * 3,
        out_specs=VMEM,
        compiler_params=limit(16),
        name="unpack",
    )(fam, rank, home)
    return out.reshape(rows)


def solution(mesh):
    in_specs = (P(("grp", "blk"), None), P(("grp", "blk")), P("grp", "blk"))
    return jax.shard_map(
        on_device, mesh=mesh, in_specs=in_specs, out_specs=P(("grp", "blk")), check_vma=False
    )
```

```python
import functools

import jax
import jax.numpy as jnp
from jax import lax
from jax.experimental import pallas as pl
from jax.experimental.pallas import tpu as pltpu
from jax.sharding import PartitionSpec as P

BF16, F32, I32 = jnp.bfloat16, jnp.float32, jnp.int32
LANES = 128
CLUSTERS = 4
NOTE = 8
VMEM = pl.BlockSpec(memory_space=pltpu.VMEM)
SMEM = pl.BlockSpec(memory_space=pltpu.SMEM)
MIB = 1 << 20


def dot_nt(a, b):
    return lax.dot_general(a, b, (((1,), (1,)), ((), ())), preferred_element_type=F32)


def iota(shape, dim):
    return lax.broadcasted_iota(I32, shape, dim)


def one_hot(match):
    return jnp.where(match, 1.0, 0.0).astype(BF16)


def digits(x):
    return [(x >> 6).astype(F32), (x & 63).astype(F32)]


def places(n, family_rows, route):
    blocks = route.shape[0]
    fam = jnp.zeros_like(route)
    for f in range(1, n):
        fam = fam + jnp.where(route >= f * family_rows, 1, 0)
    rel = route - fam * family_rows
    pad = -blocks % 16
    tall = blocks + pad
    fam_pad = jnp.concatenate([fam, jnp.full((pad, LANES), -1, I32)], axis=0) if pad else fam
    member = jnp.concatenate([jnp.where(fam_pad == f, 1.0, 0.0) for f in range(n)], axis=0)
    member_low = member.astype(BF16)
    before = one_hot(iota((LANES, LANES), 0) < iota((LANES, LANES), 1))
    within = jnp.dot(member_low, before, preferred_element_type=F32)
    totals = jnp.dot(member_low, jnp.ones((LANES, LANES), BF16), preferred_element_type=F32)
    size = n * tall
    shift = tall.bit_length() - 1
    row, col = iota((size, size), 0), iota((size, size), 1)
    above = one_hot(((row >> shift) == (col >> shift)) & (col < row))
    ranks = within + jnp.dot(above, totals.astype(BF16), preferred_element_type=F32)
    ranks = ranks * member
    rank = jnp.zeros((tall, LANES), F32)
    for f in range(n):
        rank = rank + ranks[f * tall:(f + 1) * tall]
    rank = rank.astype(I32)

    def as_row(x):
        return jnp.concatenate([x[i:i + 1] for i in range(blocks)], axis=1)

    return as_row(fam), as_row(rank), as_row(rel)


def pack(n, piece, which, grp, unit_ref, fam_row, rank_row, note_ref, outs):
    rows, width = unit_ref.shape
    pos = (fam_row ^ grp) * piece + rank_row
    for d, out in zip(which, outs):
        select = one_hot(iota((piece, rows), 0) + d * piece == pos)
        got = jnp.dot(select, unit_ref[...], preferred_element_type=F32)
        note = note_ref[grp ^ d]
        note = jnp.concatenate([note, jnp.zeros((NOTE, width - note.shape[1]), F32)], axis=1)
        out[:piece + NOTE] = jnp.concatenate([got, note], axis=0).astype(BF16)
        if out.shape[0] > piece + NOTE:
            out[piece + NOTE:] = jnp.zeros((out.shape[0] - piece - NOTE, width), BF16)


def first_kernel(n, piece, family_rows, which, here_ref, route_ref, emb_ref, *rest):
    fam_ref, rank_ref, note_ref, unit_ref = rest[:4]
    outs = rest[4:4 + len(which)]
    rows = emb_ref.shape[0]
    fam_row, rank_row, rel_row = places(n, family_rows, route_ref[...])
    fam_ref[...] = fam_row
    rank_ref[...] = rank_row
    mine = iota((n, rows), 0) == fam_row
    high, low = [jnp.where(mine, x, 0.0) for x in digits(rel_row)]
    at_rank = one_hot(iota((piece, rows), 0) == rank_row)
    slots = dot_nt(jnp.concatenate([high, low], axis=0).astype(BF16), at_rank)
    counts = jnp.zeros((NOTE - 2, piece), F32)
    spare = note_ref.shape[-1] - piece
    for f in range(n):
        note = jnp.concatenate([slots[f:f + 1], slots[n + f:n + f + 1], counts], axis=0)
        if spare:
            note = jnp.concatenate([note, jnp.zeros((NOTE, spare), F32)], axis=1)
        note_ref[f] = note

    @pl.loop(0, rows // 128)
    def _(i):
        at = pl.ds(pl.multiple_of(i * 128, 128), 128)
        x = emb_ref[at, :].astype(F32)
        total = jnp.sum(x * x, axis=1, keepdims=True)
        unit_ref[at, :] = (x * lax.rsqrt(total + 1e-06)).astype(BF16)

    pack(n, piece, which, here_ref[0], unit_ref, fam_row, rank_row, note_ref, outs)


def second_kernel(
    n, piece, which, here_ref, cluster_ref, fam_ref, rank_ref, note_ref, unit_ref, *rest
):
    *outs, token_ref, counted = rest
    token_ref[...] = jnp.zeros(token_ref.shape, F32)
    cluster = cluster_ref[...]
    counts = [jnp.zeros((2, note_ref.shape[-1]), F32)]
    for c in range(CLUSTERS - 1):
        total = jnp.sum(jnp.where(cluster <= c, 1.0, 0.0), axis=1, keepdims=True)
        counts += digits(jnp.broadcast_to(total, (1, note_ref.shape[-1])).astype(I32))
    counted[...] = note_ref[...]
    counted[here_ref[0]] = note_ref[here_ref[0]] + jnp.concatenate(counts, axis=0)
    pack(n, piece, which, here_ref[0], unit_ref, fam_ref[...], rank_ref[...], counted, outs)


def join_kernel(count, *refs):
    out_ref = refs[-1]
    for i in range(count):
        out_ref[i] = refs[i][:out_ref.shape[1]]


def stage_kernel(n, nb, piece, old, groups, side, here_ref, token_ref, *rest):
    new = [d for group in groups for d in group]
    came = range(nb) if side is None else range(side * nb // 2, (side + 1) * nb // 2)
    pieces = [
        [rest[i * len(came) + k].at[j] for k in range(len(came))]
        for i, group in enumerate(groups)
        for j in range(len(group))
    ]
    out_ref, keys, best, key_kinds, query_kinds, bounds_ref = rest[-6:]
    grp, blk = here_ref[0], here_ref[1]
    width = keys.shape[-1]
    wide = -(-piece // LANES) * LANES

    def note_of(ref):
        return ref[piece:, :wide].astype(F32)

    if not old:
        bounds = [jnp.zeros((1, piece), F32)] * (CLUSTERS - 1)
        for ref in pieces[0]:
            note = note_of(ref)[:, :piece]
            bounds = [
                b + note[2 + 2 * c:3 + 2 * c] * 64.0 + note[3 + 2 * c:4 + 2 * c]
                for c, b in enumerate(bounds)
            ]
        for c, bound in enumerate(bounds):
            bounds_ref[c] = bound
    bounds = [bounds_ref[c] for c in range(CLUSTERS - 1)]
    first = iota((8, piece), 0) == 0
    ones = jnp.where(iota((8, LANES), 0) == 0, 1.0, 0.0).astype(BF16)
    if not old:
        best[...] = jnp.full(best.shape, -1.0, F32)
    for d, refs in zip(new, pieces):
        column = grp ^ d
        for e, ref in zip(came, refs):
            keys[column, blk ^ e] = ref[:piece]
            note = note_of(ref)[:, :piece]
            slots = note[0:1] * 64.0 + note[1:2]
            kinds = jnp.zeros((1, piece), F32)
            for bound in bounds:
                kinds = kinds + jnp.where(slots >= bound, 1.0, 0.0)
            if not e:
                query_kinds[column] = kinds
            key_kinds[column * nb + (blk ^ e)] = lax.dot_general(
                jnp.where(first, kinds, 0.0).astype(BF16),
                ones,
                (((0,), (0,)), ((), ())),
                preferred_element_type=F32,
            )

    def fold(query, key, causal):
        if side is None:
            count, first_blk = nb, 0
        else:
            count = nb // 2
            first_blk = ((blk // count) ^ side) * count
        span = count * piece
        k = keys[key, pl.ds(first_blk, count)].reshape(span, width)
        scores = dot_nt(k, keys[query, blk])
        kinds = key_kinds[pl.ds(key * nb + first_blk, count)].reshape(span, LANES)
        parts = []
        for at in range(0, piece, LANES):
            w = min(LANES, piece - at)
            match = kinds[:, :w] == query_kinds[query][:, at:at + w]
            if causal:
                early = iota((span, w), 0) - iota((span, w), 1) < (blk - first_blk) * piece + at
                match = match & early
            part = jnp.where(match, scores[:, at:at + w], -1.0)
            parts.append(jnp.max(part.reshape(span // 8, 8, w), axis=0))
        folded = jnp.concatenate(parts, axis=1) if len(parts) > 1 else parts[0]
        best[query] = jnp.maximum(best[query], folded)

    def pair(a, b):
        one, two = grp ^ a, grp ^ b
        fold(jnp.maximum(one, two), jnp.minimum(one, two), False)

    if n <= 8:
        for i, a in enumerate(new):
            fold(grp ^ a, grp ^ a, True)
            for b in old + new[:i]:
                pair(a, b)
    else:
        @pl.loop(len(old), len(old) + len(new))
        def _(a):
            fold(grp ^ a, grp ^ a, True)

            @pl.loop(0, a)
            def _(b):
                pair(a, b)

    if len(old) + len(new) == n and side != 0:
        for f in range(n):
            out_ref[f] = jnp.max(best[f], axis=0, keepdims=True)


def unpack_kernel(n, piece, fam_ref, rank_ref, score_ref, out_ref):
    x = jnp.concatenate([score_ref[f] for f in range(n)], axis=0)
    high = x.astype(BF16)
    rest = x - high.astype(F32)
    mid = rest.astype(BF16)
    low = (rest - mid.astype(F32)).astype(BF16)
    rows = fam_ref.shape[1]
    at_rank = one_hot(iota((piece, rows), 0) == rank_ref[...])
    got = jnp.dot(jnp.concatenate([high, mid, low], axis=0), at_rank, preferred_element_type=F32)
    value = got[:n] + got[n:2 * n] + got[2 * n:]
    value = jnp.where(iota((n, rows), 0) == fam_ref[...], value, 0.0)
    value = jnp.sum(value, axis=0, keepdims=True)
    for i in range(out_ref.shape[0]):
        out_ref[i:i + 1] = value[:, i * LANES:(i + 1) * LANES]


def shape(*dims, kind=F32):
    return jax.ShapeDtypeStruct(dims, kind)


def send(x, axis, by):
    return lax.ppermute(x, axis, [(i, i ^ by) for i in range(lax.axis_size(axis))])


def limit(mib):
    return pltpu.CompilerParams(vmem_limit_bytes=mib * MIB)


def cost(flops):
    return pl.CostEstimate(flops=flops, bytes_accessed=0, transcendentals=0)


def on_device(embeddings, route, cluster):
    rows, width = embeddings.shape
    n, nb = lax.axis_size("grp"), lax.axis_size("blk")
    piece = rows // n
    half = n // 2
    grp, blk = lax.axis_index("grp"), lax.axis_index("blk")
    here = jnp.stack([grp, blk]).astype(I32)
    blocks = rows // LANES
    wide = -(-piece // LANES) * LANES
    one_piece = shape(piece + NOTE, width, kind=BF16)
    longer = shape(piece + 2 * NOTE, width, kind=BF16)
    kind_of = {d: longer if n == 8 and d in (2, 4, 6) else one_piece for d in range(n)}

    early = [half, 2]
    late = [d for d in range(n) if d not in early]
    fam, rank, note, unit, *packed = pl.pallas_call(
        functools.partial(first_kernel, n, piece, rows * nb, early),
        out_shape=[shape(1, rows, kind=I32)] * 2
        + [shape(n, NOTE, wide), shape(rows, width, kind=BF16)]
        + [kind_of[d] for d in early],
        in_specs=[SMEM, VMEM, VMEM],
        out_specs=[VMEM] * (4 + len(early)),
        compiler_params=limit(16),
        name="first",
    )(here, route.reshape(blocks, LANES), embeddings)
    *others, token = pl.pallas_call(
        functools.partial(second_kernel, n, piece, late),
        out_shape=[kind_of[d] for d in late] + [shape(8, LANES)],
        in_specs=[SMEM] + [VMEM] * 5,
        out_specs=[VMEM] * (len(late) + 1),
        scratch_shapes=[pltpu.VMEM((n, NOTE, wide), F32)],
        compiler_params=limit(16),
        cost_estimate=cost(8 * rows * rows * width),
        name="second",
    )(here, cluster, fam, rank, note, unit)
    sent = dict(zip(early + late, packed + others))
    own, seen, state = {0: sent[0]}, [], []

    def to_columns(*ds):
        for d in ds:
            own[d] = send(sent[d], "grp", d)

    def join(ds, later=()):
        nonlocal token
        ins = [own[d] for d in ds]
        kept = [token, *later]
        joined = [shape(len(ins), *one_piece.shape, kind=BF16)] if ins else []
        token, *rest = pl.pallas_call(
            functools.partial(join_kernel, len(ins)),
            out_shape=[jax.ShapeDtypeStruct(x.shape, x.dtype) for x in kept] + joined,
            in_specs=[VMEM] * (len(ins) + len(kept)),
            out_specs=[VMEM] * (len(kept) + len(joined)),
            input_output_aliases={len(ins) + i: i for i in range(len(kept))},
            compiler_params=limit(4),
            cost_estimate=cost(0),
            name="join",
        )(*ins, *kept)
        return rest[len(later):] + rest[:len(later)]

    def stage(*groups, side=None):
        nonlocal token, seen, state
        kept = [
            shape(n, nb, piece, width, kind=BF16),
            shape(n, 8, piece),
            shape(n * nb, piece, LANES),
            shape(n, 1, piece),
            shape(CLUSTERS - 1, 1, piece),
        ]
        args = [here, token]
        for _, *four in groups:
            args += four
        args += list(state)
        ds = [list(group[0]) for group in groups]
        now = seen + sum(ds, [])
        outs = [shape(8, LANES)] + ([shape(n, 1, piece)] if len(now) == n and side != 0 else []) + kept
        alias = {1: 0}
        if seen:
            alias |= {len(args) - 5 + i: len(outs) - 5 + i for i in range(5)}
        folds = sum(range(len(seen) + 1, len(now) + 1))
        token, *state = pl.pallas_call(
            functools.partial(stage_kernel, n, nb, piece, seen, ds, side),
            out_shape=outs,
            in_specs=[SMEM] + [VMEM] * (len(args) - 1),
            out_specs=[VMEM] * len(outs),
            input_output_aliases=alias,
            compiler_params=limit(12),
            cost_estimate=cost(folds * 4 * piece * piece * nb * width),
            name="stage",
        )(*args)
        seen = seen if side == 0 else now

    if n == 8:
        to_columns(4, 2)
        m0 = own[0].reshape(1, *one_piece.shape)
        y0, c0 = send(m0, "blk", 2), send(m0, "blk", 1)
        m1, y0, c0, sent[5], sent[3] = join((4, 2), [y0, c0, sent[5], sent[3]])
        to_columns(5, 3)
        y1, c1, x0 = send(m1, "blk", 2), send(m1, "blk", 1), send(y0, "blk", 1)
        m2, y1, c1, x0, sent[6], sent[1] = join((5, 3), [y1, c1, x0, sent[6], sent[1]])
        to_columns(6, 1)
        y2, c2, x1 = send(m2, "blk", 2), send(m2, "blk", 1), send(y1, "blk", 1)
        m3, y2, c2, x1, sent[7] = join((6, 1), [y2, c2, x1, sent[7]])
        to_columns(7)
        y3, c3, x2 = send(m3, "blk", 2), send(m3, "blk", 1), send(y2, "blk", 1)
        stage(((0,), m0, c0, y0, x0), ((4, 2), m1, c1, y1, x1), ((5, 3), m2, c2, y2, x2))
        m4, y3, c3 = join((7,), [y3, c3])
        y4, c4, x3 = send(m4, "blk", 2), send(m4, "blk", 1), send(y3, "blk", 1)
        stage(((6, 1), m3, c3, y3, x3))
        stage(((7,), m4, c4), side=0)
        (y4,) = join((), [y4])
        stage(((7,), y4, send(y4, "blk", 1)), side=1)
    else:
        to_columns(*range(1, n))
        for lo in range(0, n, 8):
            ds = range(lo, lo + 8)
            (m,) = join(ds)
            y = send(m, "blk", 2)
            stage((ds, m, send(m, "blk", 1), y, send(y, "blk", 1)))
    scores = state[0]

    home = lax.all_to_all(scores, "grp", split_axis=0, concat_axis=0, tiled=True)
    out = pl.pallas_call(
        functools.partial(unpack_kernel, n, piece),
        out_shape=shape(blocks, LANES),
        in_specs=[VMEM] * 3,
        out_specs=VMEM,
        compiler_params=limit(16),
        name="unpack",
    )(fam, rank, home)
    return out.reshape(rows)


def solution(mesh):
    in_specs = (P(("grp", "blk"), None), P(("grp", "blk")), P("grp", "blk"))
    return jax.shard_map(
        on_device, mesh=mesh, in_specs=in_specs, out_specs=P(("grp", "blk")), check_vma=False
    )
```

```python
import functools

import jax
import jax.numpy as jnp
from jax import lax
from jax.experimental import pallas as pl
from jax.experimental.pallas import tpu as pltpu
from jax.sharding import PartitionSpec as P

BF16, F32, I32 = jnp.bfloat16, jnp.float32, jnp.int32
LANES = 128
CLUSTERS = 4
NOTE = 8
VMEM = pl.BlockSpec(memory_space=pltpu.VMEM)
SMEM = pl.BlockSpec(memory_space=pltpu.SMEM)
MIB = 1 << 20


def dot_nt(a, b):
    return lax.dot_general(a, b, (((1,), (1,)), ((), ())), preferred_element_type=F32)


def iota(shape, dim):
    return lax.broadcasted_iota(I32, shape, dim)


def one_hot(match):
    return jnp.where(match, 1.0, 0.0).astype(BF16)


def digits(x):
    return [(x >> 6).astype(F32), (x & 63).astype(F32)]


def places(n, family_rows, route):
    blocks = route.shape[0]
    fam = jnp.zeros_like(route)
    for f in range(1, n):
        fam = fam + jnp.where(route >= f * family_rows, 1, 0)
    rel = route - fam * family_rows
    pad = -blocks % 16
    tall = blocks + pad
    fam_pad = jnp.concatenate([fam, jnp.full((pad, LANES), -1, I32)], axis=0) if pad else fam
    member = jnp.concatenate([jnp.where(fam_pad == f, 1.0, 0.0) for f in range(n)], axis=0)
    member_low = member.astype(BF16)
    before = one_hot(iota((LANES, LANES), 0) < iota((LANES, LANES), 1))
    within = jnp.dot(member_low, before, preferred_element_type=F32)
    totals = jnp.dot(member_low, jnp.ones((LANES, LANES), BF16), preferred_element_type=F32)
    size = n * tall
    shift = tall.bit_length() - 1
    row, col = iota((size, size), 0), iota((size, size), 1)
    above = one_hot(((row >> shift) == (col >> shift)) & (col < row))
    ranks = within + jnp.dot(above, totals.astype(BF16), preferred_element_type=F32)
    ranks = ranks * member
    rank = jnp.zeros((tall, LANES), F32)
    for f in range(n):
        rank = rank + ranks[f * tall:(f + 1) * tall]
    rank = rank.astype(I32)

    def as_row(x):
        return jnp.concatenate([x[i:i + 1] for i in range(blocks)], axis=1)

    return as_row(fam), as_row(rank), as_row(rel)


def pack(n, piece, which, grp, unit_ref, fam_row, rank_row, note_ref, outs):
    rows, width = unit_ref.shape
    pos = (fam_row ^ grp) * piece + rank_row
    for d, out in zip(which, outs):
        select = one_hot(iota((piece, rows), 0) + d * piece == pos)
        got = jnp.dot(select, unit_ref[...], preferred_element_type=F32)
        note = note_ref[grp ^ d]
        note = jnp.concatenate([note, jnp.zeros((NOTE, width - note.shape[1]), F32)], axis=1)
        out[:piece + NOTE] = jnp.concatenate([got, note], axis=0).astype(BF16)
        if out.shape[0] > piece + NOTE:
            out[piece + NOTE:] = jnp.zeros((out.shape[0] - piece - NOTE, width), BF16)


def first_kernel(n, piece, family_rows, which, here_ref, route_ref, emb_ref, *rest):
    fam_ref, rank_ref, note_ref, unit_ref = rest[:4]
    outs = rest[4:4 + len(which)]
    rows = emb_ref.shape[0]
    fam_row, rank_row, rel_row = places(n, family_rows, route_ref[...])
    fam_ref[...] = fam_row
    rank_ref[...] = rank_row
    mine = iota((n, rows), 0) == fam_row
    high, low = [jnp.where(mine, x, 0.0) for x in digits(rel_row)]
    at_rank = one_hot(iota((piece, rows), 0) == rank_row)
    slots = dot_nt(jnp.concatenate([high, low], axis=0).astype(BF16), at_rank)
    counts = jnp.zeros((NOTE - 2, piece), F32)
    spare = note_ref.shape[-1] - piece
    for f in range(n):
        note = jnp.concatenate([slots[f:f + 1], slots[n + f:n + f + 1], counts], axis=0)
        if spare:
            note = jnp.concatenate([note, jnp.zeros((NOTE, spare), F32)], axis=1)
        note_ref[f] = note

    @pl.loop(0, rows // 128)
    def _(i):
        at = pl.ds(pl.multiple_of(i * 128, 128), 128)
        x = emb_ref[at, :].astype(F32)
        total = jnp.sum(x * x, axis=1, keepdims=True)
        unit_ref[at, :] = (x * lax.rsqrt(total + 1e-06)).astype(BF16)

    pack(n, piece, which, here_ref[0], unit_ref, fam_row, rank_row, note_ref, outs)


def second_kernel(
    n, piece, which, here_ref, cluster_ref, fam_ref, rank_ref, note_ref, unit_ref, *rest
):
    *outs, token_ref, counted = rest
    token_ref[...] = jnp.zeros(token_ref.shape, F32)
    cluster = cluster_ref[...]
    counts = [jnp.zeros((2, note_ref.shape[-1]), F32)]
    for c in range(CLUSTERS - 1):
        total = jnp.sum(jnp.where(cluster <= c, 1.0, 0.0), axis=1, keepdims=True)
        counts += digits(jnp.broadcast_to(total, (1, note_ref.shape[-1])).astype(I32))
    counted[...] = note_ref[...]
    counted[here_ref[0]] = note_ref[here_ref[0]] + jnp.concatenate(counts, axis=0)
    pack(n, piece, which, here_ref[0], unit_ref, fam_ref[...], rank_ref[...], counted, outs)


def join_kernel(count, *refs):
    out_ref = refs[-1]
    for i in range(count):
        out_ref[i] = refs[i][:out_ref.shape[1]]


def stage_kernel(n, nb, piece, old, groups, side, here_ref, token_ref, *rest):
    new = [d for group in groups for d in group]
    came = range(nb) if side is None else range(side * nb // 2, (side + 1) * nb // 2)
    pieces = [
        [rest[i * len(came) + k].at[j] for k in range(len(came))]
        for i, group in enumerate(groups)
        for j in range(len(group))
    ]
    out_ref, keys, best, key_kinds, query_kinds, bounds_ref = rest[-6:]
    grp, blk = here_ref[0], here_ref[1]
    width = keys.shape[-1]
    wide = -(-piece // LANES) * LANES

    def note_of(ref):
        return ref[piece:, :wide].astype(F32)

    if not old:
        bounds = [jnp.zeros((1, piece), F32)] * (CLUSTERS - 1)
        for ref in pieces[0]:
            note = note_of(ref)[:, :piece]
            bounds = [
                b + note[2 + 2 * c:3 + 2 * c] * 64.0 + note[3 + 2 * c:4 + 2 * c]
                for c, b in enumerate(bounds)
            ]
        for c, bound in enumerate(bounds):
            bounds_ref[c] = bound
    bounds = [bounds_ref[c] for c in range(CLUSTERS - 1)]
    first = iota((8, piece), 0) == 0
    ones = jnp.where(iota((8, LANES), 0) == 0, 1.0, 0.0).astype(BF16)
    if not old:
        best[...] = jnp.full(best.shape, -1.0, F32)
    for d, refs in zip(new, pieces):
        column = grp ^ d
        for e, ref in zip(came, refs):
            keys[column, blk ^ e] = ref[:piece]
            note = note_of(ref)[:, :piece]
            slots = note[0:1] * 64.0 + note[1:2]
            kinds = jnp.zeros((1, piece), F32)
            for bound in bounds:
                kinds = kinds + jnp.where(slots >= bound, 1.0, 0.0)
            if not e:
                query_kinds[column] = kinds
            key_kinds[column * nb + (blk ^ e)] = lax.dot_general(
                jnp.where(first, kinds, 0.0).astype(BF16),
                ones,
                (((0,), (0,)), ((), ())),
                preferred_element_type=F32,
            )

    def fold(query, key, causal):
        if side is None:
            count, first_blk = nb, 0
        else:
            count = nb // 2
            first_blk = ((blk // count) ^ side) * count
        span = count * piece
        k = keys[key, pl.ds(first_blk, count)].reshape(span, width)
        scores = dot_nt(k, keys[query, blk])
        kinds = key_kinds[pl.ds(key * nb + first_blk, count)].reshape(span, LANES)
        parts = []
        for at in range(0, piece, LANES):
            w = min(LANES, piece - at)
            match = kinds[:, :w] == query_kinds[query][:, at:at + w]
            if causal:
                early = iota((span, w), 0) - iota((span, w), 1) < (blk - first_blk) * piece + at
                match = match & early
            part = jnp.where(match, scores[:, at:at + w], -1.0)
            parts.append(jnp.max(part.reshape(span // 8, 8, w), axis=0))
        folded = jnp.concatenate(parts, axis=1) if len(parts) > 1 else parts[0]
        best[query] = jnp.maximum(best[query], folded)

    def pair(a, b):
        one, two = grp ^ a, grp ^ b
        fold(jnp.maximum(one, two), jnp.minimum(one, two), False)

    if n <= 8:
        for i, a in enumerate(new):
            fold(grp ^ a, grp ^ a, True)
            for b in old + new[:i]:
                pair(a, b)
    else:
        @pl.loop(len(old), len(old) + len(new))
        def _(a):
            fold(grp ^ a, grp ^ a, True)

            @pl.loop(0, a)
            def _(b):
                pair(a, b)

    if len(old) + len(new) == n and side != 0:
        for f in range(n):
            out_ref[f] = jnp.max(best[f], axis=0, keepdims=True)


def unpack_kernel(n, piece, fam_ref, rank_ref, score_ref, out_ref):
    x = jnp.concatenate([score_ref[f] for f in range(n)], axis=0)
    high = x.astype(BF16)
    rest = x - high.astype(F32)
    mid = rest.astype(BF16)
    low = (rest - mid.astype(F32)).astype(BF16)
    rows = fam_ref.shape[1]
    at_rank = one_hot(iota((piece, rows), 0) == rank_ref[...])
    got = jnp.dot(jnp.concatenate([high, mid, low], axis=0), at_rank, preferred_element_type=F32)
    value = got[:n] + got[n:2 * n] + got[2 * n:]
    value = jnp.where(iota((n, rows), 0) == fam_ref[...], value, 0.0)
    value = jnp.sum(value, axis=0, keepdims=True)
    for i in range(out_ref.shape[0]):
        out_ref[i:i + 1] = value[:, i * LANES:(i + 1) * LANES]


def shape(*dims, kind=F32):
    return jax.ShapeDtypeStruct(dims, kind)


def send(x, axis, by):
    return lax.ppermute(x, axis, [(i, i ^ by) for i in range(lax.axis_size(axis))])


def limit(mib):
    return pltpu.CompilerParams(vmem_limit_bytes=mib * MIB)


def cost(flops):
    return pl.CostEstimate(flops=flops, bytes_accessed=0, transcendentals=0)


def on_device(embeddings, route, cluster):
    rows, width = embeddings.shape
    n, nb = lax.axis_size("grp"), lax.axis_size("blk")
    piece = rows // n
    half = n // 2
    grp, blk = lax.axis_index("grp"), lax.axis_index("blk")
    here = jnp.stack([grp, blk]).astype(I32)
    blocks = rows // LANES
    wide = -(-piece // LANES) * LANES
    one_piece = shape(piece + NOTE, width, kind=BF16)
    longer = shape(piece + 2 * NOTE, width, kind=BF16)
    kind_of = {d: longer if n == 8 and d in (2, 4, 6) else one_piece for d in range(n)}

    early = [half, 2]
    late = [d for d in range(n) if d not in early]
    fam, rank, note, unit, *packed = pl.pallas_call(
        functools.partial(first_kernel, n, piece, rows * nb, early),
        out_shape=[shape(1, rows, kind=I32)] * 2
        + [shape(n, NOTE, wide), shape(rows, width, kind=BF16)]
        + [kind_of[d] for d in early],
        in_specs=[SMEM, VMEM, VMEM],
        out_specs=[VMEM] * (4 + len(early)),
        compiler_params=limit(16),
        name="first",
    )(here, route.reshape(blocks, LANES), embeddings)
    *others, token = pl.pallas_call(
        functools.partial(second_kernel, n, piece, late),
        out_shape=[kind_of[d] for d in late] + [shape(8, LANES)],
        in_specs=[SMEM] + [VMEM] * 5,
        out_specs=[VMEM] * (len(late) + 1),
        scratch_shapes=[pltpu.VMEM((n, NOTE, wide), F32)],
        compiler_params=limit(16),
        cost_estimate=cost(8 * rows * rows * width),
        name="second",
    )(here, cluster, fam, rank, note, unit)
    sent = dict(zip(early + late, packed + others))
    own, seen, state = {0: sent[0]}, [], []

    def to_columns(*ds):
        for d in ds:
            own[d] = send(sent[d], "grp", d)

    def join(ds, later=()):
        nonlocal token
        ins = [own[d] for d in ds]
        kept = [token, *later]
        joined = [shape(len(ins), *one_piece.shape, kind=BF16)] if ins else []
        token, *rest = pl.pallas_call(
            functools.partial(join_kernel, len(ins)),
            out_shape=[jax.ShapeDtypeStruct(x.shape, x.dtype) for x in kept] + joined,
            in_specs=[VMEM] * (len(ins) + len(kept)),
            out_specs=[VMEM] * (len(kept) + len(joined)),
            input_output_aliases={len(ins) + i: i for i in range(len(kept))},
            compiler_params=limit(4),
            cost_estimate=cost(0),
            name="join",
        )(*ins, *kept)
        return rest[len(later):] + rest[:len(later)]

    def stage(*groups, side=None):
        nonlocal token, seen, state
        kept = [
            shape(n, nb, piece, width, kind=BF16),
            shape(n, 8, piece),
            shape(n * nb, piece, LANES),
            shape(n, 1, piece),
            shape(CLUSTERS - 1, 1, piece),
        ]
        args = [here, token]
        for _, *four in groups:
            args += four
        args += list(state)
        ds = [list(group[0]) for group in groups]
        now = seen + sum(ds, [])
        outs = [shape(8, LANES)] + ([shape(n, 1, piece)] if len(now) == n and side != 0 else []) + kept
        alias = {1: 0}
        if seen:
            alias |= {len(args) - 5 + i: len(outs) - 5 + i for i in range(5)}
        folds = sum(range(len(seen) + 1, len(now) + 1))
        token, *state = pl.pallas_call(
            functools.partial(stage_kernel, n, nb, piece, seen, ds, side),
            out_shape=outs,
            in_specs=[SMEM] + [VMEM] * (len(args) - 1),
            out_specs=[VMEM] * len(outs),
            input_output_aliases=alias,
            compiler_params=limit(12),
            cost_estimate=cost(folds * 4 * piece * piece * nb * width),
            name="stage",
        )(*args)
        seen = seen if side == 0 else now

    if n == 8:
        to_columns(4, 2)
        m0 = own[0].reshape(1, *one_piece.shape)
        y0, c0 = send(m0, "blk", 2), send(m0, "blk", 1)
        m1, y0, c0, sent[5], sent[1] = join((4, 2), [y0, c0, sent[5], sent[1]])
        to_columns(5, 1)
        y1, c1, x0 = send(m1, "blk", 2), send(m1, "blk", 1), send(y0, "blk", 1)
        m2, y1, c1, x0, sent[6], sent[3] = join((5, 1), [y1, c1, x0, sent[6], sent[3]])
        to_columns(6, 3)
        y2, c2, x1 = send(m2, "blk", 2), send(m2, "blk", 1), send(y1, "blk", 1)
        m3, y2, c2, x1, sent[7] = join((6, 3), [y2, c2, x1, sent[7]])
        to_columns(7)
        y3, c3, x2 = send(m3, "blk", 2), send(m3, "blk", 1), send(y2, "blk", 1)
        stage(((0,), m0, c0, y0, x0), ((4, 2), m1, c1, y1, x1), ((5, 1), m2, c2, y2, x2))
        m4, y3, c3 = join((7,), [y3, c3])
        y4, c4, x3 = send(m4, "blk", 2), send(m4, "blk", 1), send(y3, "blk", 1)
        stage(((6, 3), m3, c3, y3, x3))
        stage(((7,), m4, c4), side=0)
        (y4,) = join((), [y4])
        stage(((7,), y4, send(y4, "blk", 1)), side=1)
    else:
        to_columns(*range(1, n))
        for lo in range(0, n, 8):
            ds = range(lo, lo + 8)
            (m,) = join(ds)
            y = send(m, "blk", 2)
            stage((ds, m, send(m, "blk", 1), y, send(y, "blk", 1)))
    scores = state[0]

    home = lax.all_to_all(scores, "grp", split_axis=0, concat_axis=0, tiled=True)
    out = pl.pallas_call(
        functools.partial(unpack_kernel, n, piece),
        out_shape=shape(blocks, LANES),
        in_specs=[VMEM] * 3,
        out_specs=VMEM,
        compiler_params=limit(16),
        name="unpack",
    )(fam, rank, home)
    return out.reshape(rows)


def solution(mesh):
    in_specs = (P(("grp", "blk"), None), P(("grp", "blk")), P("grp", "blk"))
    return jax.shard_map(
        on_device, mesh=mesh, in_specs=in_specs, out_specs=P(("grp", "blk")), check_vma=False
    )
```
